128 devices in a mesh: gz: 16 (over y_lo, x, core), head: 2 (over y_hi), tile: 4 (over z).
Axes of the slice: x: 4, y: 4 (y_hi: 2, y_lo: 2; y = y_hi * 2 + y_lo), z: 4, core: 2. Of those that a mesh axis runs over, the one named last changes fastest.
Arguments:
- nodes_in: bfloat16 [524288, 256], P(('gz', 'tile')), may hold values from -6 to 6
- cotangent: bfloat16 [524288, 256], P(('gz', 'tile')), may hold values from -6 to 6
- w_query: bfloat16 [256, 256], P(None, 'head'), may hold values from -0.375 to 0.375
- w_key: bfloat16 [256, 256], P(None, 'head'), may hold values from -0.375 to 0.375
- w_value: bfloat16 [256, 256], P(None, 'head'), may hold values from -0.375 to 0.375
- w_out: bfloat16 [256, 256], P('head'), may hold values from -0.375 to 0.375
- counts: int32 [4096], replicated, may hold values from 4 to 128
Outputs:
- output: bfloat16 [524288, 256], P(('gz', 'tile'), 'head')
- grad_nodes: bfloat16 [524288, 256], P(('gz', 'tile'), 'head')
- grad_query: float32 [256, 256], P(None, 'head')
- grad_key: float32 [256, 256], P(None, 'head')
- grad_value: float32 [256, 256], P(None, 'head')
- grad_out: float32 [256, 256], P('head')
The draws below stay inside these ranges and needn't reach their ends.
Inputs may be any that keep to these rules, and one draw needn't show every extreme that they name: counts[b] is how many of the nodes b * 128 to (b + 1) * 128 - 1 are valid; the valid ones are the first of them.
All inputs are finite; a program needn't handle non-finite values.
Results may differ from the reference program's by a relative error of at most 0.012.
The reference program's roundings to bfloat16 on the way count: a program that leaves them out, or rounds other values in their place, can miss the bound.
Values may be sent and summed in bfloat16 or wider, within the bound.
No kernel may reach another device: no remote copies, remote signals or barrier semaphores. Data moves between devices by JAX's collectives and lax.ppermute only.
A program may use at most 128 MiB of HBM per device.

```python
import math
import jax
import jax.numpy as jnp
import numpy as np
from jax import lax

C = 256
HEADS = 8
WINDOW = 128
HEAD_DIM = 32
HEADS_DEV = 4
NODES = 524288
N_HEAD = 2


def touch_ends(values, rng, low, top_value):
    longest = values.shape.index(max(values.shape))
    spots = []
    for shift in (0, 1):
        where = [jax.random.randint(jax.random.fold_in(rng, axis), (), 0, length) for axis, length in enumerate(values.shape)]
        where[longest] = (where[longest] + shift) % values.shape[longest]
        spots.append(tuple(where))
    return values.at[spots[0]].set(low).at[spots[1]].set(top_value)


def shard_levels(rng, extent, shards, least, top_value):
    factor_of, own = 1.0, jax.random.fold_in(rng, 6)
    for position, blocks in shards:
        heights = jnp.exp(jax.random.uniform(jax.random.fold_in(own, position), (blocks,), jnp.float32, least / len(shards), top_value / len(shards)))
        factor_of = factor_of * jnp.repeat(heights, extent[position] // blocks).reshape([-1 if axis == position else 1 for axis in range(len(extent))])
    return factor_of


def bell_draw(own_key, shape, deviation, reach, pieces=(), kind=jnp.bfloat16):
    values = deviation * jax.random.normal(own_key, shape, jnp.float32)
    if pieces:
        values = values * shard_levels(own_key, shape, pieces, -0.22, 0.18)
    return jnp.clip(values, -reach, reach).astype(kind)


def setup_inputs(seed: int = 0) -> dict:
    key_list = jax.random.split(jax.random.key(seed), 8)
    return {
        "nodes_in": bell_draw(key_list[0], (NODES, C), 1.0, 6.0, ((0, 64),)),
        "cotangent": bell_draw(key_list[1], (NODES, C), 1.0, 6.0, ((0, 64),)),
        "w_query": bell_draw(key_list[2], (C, C), C ** -0.5, 0.375, ((1, 2),)),
        "w_key": bell_draw(key_list[3], (C, C), C ** -0.5, 0.375, ((1, 2),)),
        "w_value": bell_draw(key_list[4], (C, C), C ** -0.5, 0.375, ((1, 2),)),
        "w_out": bell_draw(key_list[5], (C, C), C ** -0.5, 0.375, ((0, 2),)),
        "counts": touch_ends(jax.random.randint(key_list[6], (NODES // WINDOW,), 4, WINDOW + 1), jax.random.fold_in(key_list[6], 1), 4, WINDOW).astype(jnp.int32),
    }


def window_core(queries, key_block, values, valid_keys, dcontext, score_scale):
    scores = jnp.einsum("whqe,whke->whqk", queries.astype(jnp.float32), key_block.astype(jnp.float32)) * score_scale
    weights = jnp.exp(scores) * valid_keys[:, None, None, :]
    attention = weights / jnp.sum(weights, axis=-1, keepdims=True)
    attention_low = lax.optimization_barrier(attention.astype(jnp.bfloat16)).astype(jnp.float32)
    context = jnp.einsum("whqk,whke->whqe", attention_low, values.astype(jnp.float32)).astype(jnp.bfloat16)
    dattention = jnp.einsum("whqe,whke->whqk", dcontext.astype(jnp.float32), values.astype(jnp.float32))
    center = jnp.sum(attention * dattention, axis=-1, keepdims=True)
    dscores = lax.optimization_barrier((attention * (dattention - center)).astype(jnp.bfloat16)).astype(jnp.float32)
    dvalues = jnp.einsum("whqk,whqe->whke", attention_low, dcontext.astype(jnp.float32)).astype(jnp.bfloat16)
    dqueries = (score_scale * jnp.einsum("whqk,whke->whqe", dscores, key_block.astype(jnp.float32))).astype(jnp.bfloat16)
    key_grads = (score_scale * jnp.einsum("whqk,whqe->whke", dscores, queries.astype(jnp.float32))).astype(jnp.bfloat16)
    return context, dqueries, key_grads, dvalues


def to_windows(array, dilation):
    length, columns = array.shape
    head_count = columns // HEAD_DIM
    shaped = array.reshape(length // (WINDOW * dilation), WINDOW, dilation, head_count, HEAD_DIM)
    return shaped.transpose(0, 2, 3, 1, 4).reshape(-1, head_count, WINDOW, HEAD_DIM)


def mask_windows(valid_rows, dilation):
    length = valid_rows.shape[0]
    shaped = valid_rows.reshape(length // (WINDOW * dilation), WINDOW, dilation)
    return shaped.transpose(0, 2, 1).reshape(-1, WINDOW)


def from_windows(array, dilation, length):
    head_count = array.shape[1]
    shaped = array.reshape(length // (WINDOW * dilation), dilation, head_count, WINDOW, HEAD_DIM)
    return shaped.transpose(0, 3, 1, 2, 4).reshape(length, head_count * HEAD_DIM)


def dilated(queries, key_block, values, dcontext, valid, dilation):
    total = queries.shape[0]
    shift = (WINDOW // 2) * dilation
    score_scale = HEAD_DIM ** -0.5
    windowed = [to_windows(jnp.roll(array, -shift, axis=0), dilation) for array in (queries, key_block, values, dcontext)]
    valid_win = mask_windows(jnp.roll(valid, -shift, axis=0), dilation)
    window_count = valid_win.shape[0]
    block = math.gcd(64, window_count)

    def blocked(array):
        return array.reshape((window_count // block, block) + array.shape[1:])

    def per_block(group):
        return window_core(group[0], group[1], group[2], group[3], group[4], score_scale)

    stacked = (blocked(windowed[0]), blocked(windowed[1]), blocked(windowed[2]), blocked(valid_win), blocked(windowed[3]))
    results = lax.map(per_block, stacked)
    outputs = []
    for result in results:
        flat = result.reshape((window_count,) + result.shape[2:])
        outputs.append(jnp.roll(from_windows(flat, dilation, total), shift, axis=0))
    return outputs


def reference(nodes_in, cotangent, w_query, w_key, w_value, w_out, counts):
    total = nodes_in.shape[0]
    valid = (jnp.arange(WINDOW, dtype=jnp.int32)[None, :] < counts[:, None]).astype(jnp.float32).reshape(total)
    queries = jnp.dot(nodes_in, w_query, preferred_element_type=jnp.float32).astype(jnp.bfloat16)
    key_rows = jnp.dot(nodes_in, w_key, preferred_element_type=jnp.float32).astype(jnp.bfloat16)
    values = jnp.dot(nodes_in, w_value, preferred_element_type=jnp.float32).astype(jnp.bfloat16)
    masked_cot = cotangent * valid.astype(jnp.bfloat16)[:, None]
    dcontext = jnp.dot(masked_cot, w_out.T, preferred_element_type=jnp.float32).astype(jnp.bfloat16)
    per_device = HEADS_DEV
    near_heads = [head_id for head_id in range(HEADS) if head_id % per_device < per_device // 2]
    far_heads = [head_id for head_id in range(HEADS) if head_id % per_device >= per_device // 2]
    near_columns = np.concatenate([np.arange(head_id * HEAD_DIM, (head_id + 1) * HEAD_DIM) for head_id in near_heads])
    far_columns = np.concatenate([np.arange(head_id * HEAD_DIM, (head_id + 1) * HEAD_DIM) for head_id in far_heads])
    near_out = dilated(queries[:, near_columns], key_rows[:, near_columns], values[:, near_columns], dcontext[:, near_columns], valid, 1)
    far_out = dilated(queries[:, far_columns], key_rows[:, far_columns], values[:, far_columns], dcontext[:, far_columns], valid, 4)
    merged = []
    for near_part, far_part in zip(near_out, far_out):
        whole = jnp.zeros((total, C), jnp.bfloat16)
        merged.append(whole.at[:, near_columns].set(near_part).at[:, far_columns].set(far_part))
    context, dqueries, key_grads, dvalues = merged
    output = (valid[:, None] * jnp.dot(context, w_out, preferred_element_type=jnp.float32)).astype(jnp.bfloat16)
    group_width = C // N_HEAD
    summed = jnp.zeros((total, C), jnp.float32)
    for group in range(N_HEAD):
        low = group * group_width
        high = low + group_width
        partial_value = jnp.dot(dqueries[:, low:high], w_query[:, low:high].T, preferred_element_type=jnp.float32)
        partial_value = partial_value + jnp.dot(key_grads[:, low:high], w_key[:, low:high].T, preferred_element_type=jnp.float32)
        partial_value = partial_value + jnp.dot(dvalues[:, low:high], w_value[:, low:high].T, preferred_element_type=jnp.float32)
        summed = summed + lax.optimization_barrier(partial_value.astype(jnp.bfloat16)).astype(jnp.float32)
    grad_nodes = summed.astype(jnp.bfloat16)
    norm = float(total) ** -0.5
    grad_query = jnp.dot(nodes_in.T, dqueries, preferred_element_type=jnp.float32) * norm
    grad_key = jnp.dot(nodes_in.T, key_grads, preferred_element_type=jnp.float32) * norm
    grad_value = jnp.dot(nodes_in.T, dvalues, preferred_element_type=jnp.float32) * norm
    grad_out = jnp.dot(context.T, masked_cot, preferred_element_type=jnp.float32) * norm
    return (output, grad_nodes, grad_query, grad_key, grad_value, grad_out)
```

```python
import math

import jax
import jax.numpy as jnp
from jax import lax
from jax.experimental import pallas as pl
from jax.experimental.pallas import tpu as pltpu
from jax.sharding import PartitionSpec as P

HEADS = 8
WINDOW = 128
HALO = 256
GROUP = 512
HEAD_DIM = 32
SCALE = HEAD_DIM ** (-0.5)
EXP2_SCALE = SCALE * math.log2(math.e)
BF = jnp.bfloat16
F32 = jnp.float32


def mm(a, b):
    return jnp.dot(a, b, preferred_element_type=F32)


def mm_nt(a, b):
    return lax.dot_general(a, b, (((1,), (1,)), ((), ())), preferred_element_type=F32)


def head_spread(block):
    lane_head = lax.broadcasted_iota(jnp.int32, block.shape, 1) // HEAD_DIM
    zero = jnp.zeros_like(block)
    return jnp.concatenate([jnp.where(lane_head == h, block, zero) for h in range(4)], 0)


def windows_core(loaded, masks):
    spread_q = [head_spread(q) for q, k, v, d in loaded]
    spread_d = [head_spread(d) for q, k, v, d in loaded]
    scores = [mm_nt(w[1], sq) for w, sq in zip(loaded, spread_q)]
    datt = [mm_nt(w[2], sd) for w, sd in zip(loaded, spread_d)]
    low, dsc = [], []
    for s, da, mask in zip(scores, datt, masks):
        low_parts, dsc_parts = [], []
        for h in range(4):
            cols = slice(h * WINDOW, (h + 1) * WINDOW)
            e = jnp.where(mask, jnp.exp2(s[:, cols] * EXP2_SCALE), 0.0)
            a = e * (1.0 / jnp.sum(e, axis=0, keepdims=True))
            d = da[:, cols]
            center = jnp.sum(a * d, axis=0, keepdims=True)
            low_parts.append(a.astype(BF))
            dsc_parts.append((a * (d - center)).astype(BF))
        low.append(low_parts)
        dsc.append(dsc_parts)
    results = []
    for (q, k, v, d), sq, sd, lw, ds in zip(loaded, spread_q, spread_d, low, dsc):
        lw_all = jnp.concatenate(lw, 1)
        ds_all = jnp.concatenate(ds, 1)
        dv = mm(lw_all, sd)
        dk = mm(ds_all, sq) * SCALE
        k_t, v_t = k.T, v.T
        ctx_t, dq_t = [], []
        for pair in range(2):
            rows = slice(pair * 64, pair * 64 + 64)
            cols = slice(pair * 256, pair * 256 + 256)
            c2 = mm(v_t[rows], lw_all[:, cols])
            q2 = mm(k_t[rows], ds_all[:, cols])
            ctx_t += [c2[:32, :128], c2[32:, 128:]]
            dq_t += [q2[:32, :128], q2[32:, 128:]]
        ctx = jnp.concatenate(ctx_t, 0).T
        dq = jnp.concatenate(dq_t, 0).T * SCALE
        results.append((ctx, dq, dk, dv))
    return results


def local_kernel(rows, use_halo, norm, *refs):
    meta, counts = refs[:2]
    refs = refs[2:]
    if use_halo:
        x_hbm, c_hbm, halo_hbm, own_ref, oth_ref, g_in = refs[:6]
        refs = refs[6:]
    else:
        x_hbm, c_hbm, own_ref, oth_ref = refs[:4]
        refs = refs[4:]
    (out_keep, out_send, gn_keep, gn_send, g_out) = refs[:5]
    (xs, cs, near_in, near_out, far_out, far_stage, far_res, wqkv, wqkv_t, wout_t, wout_p, gacc, gacc_o, sems) = refs[5:]
    ext = rows + 2 * HALO
    first_block = meta[0]
    side = meta[1]
    src = pl.multiple_of(meta[2], HALO)
    block_mask = counts.shape[0]

    def count_of(block):
        return counts[lax.rem(first_block + block, block_mask)]

    copies = []
    if use_halo:
        main = ext - HALO
        dst = pl.multiple_of((1 - side) * HALO, HALO)
        hdst = pl.multiple_of(side * main, HALO)
        width = xs.shape[1]
        copies.append(pltpu.make_async_copy(x_hbm.at[pl.ds(src, main)], xs.at[pl.ds(dst, main)], sems.at[0]))
        copies.append(pltpu.make_async_copy(c_hbm.at[pl.ds(src, main)], cs.at[pl.ds(dst, main)], sems.at[1]))
        copies.append(pltpu.make_async_copy(halo_hbm.at[:, pl.ds(0, width)], xs.at[pl.ds(hdst, HALO)], sems.at[2]))
        copies.append(pltpu.make_async_copy(halo_hbm.at[:, pl.ds(width, width)], cs.at[pl.ds(hdst, HALO)], sems.at[3]))
    else:
        copies.append(pltpu.make_async_copy(x_hbm.at[pl.ds(src, ext)], xs, sems.at[0]))
        copies.append(pltpu.make_async_copy(c_hbm.at[pl.ds(src, ext)], cs, sems.at[1]))
    for copy in copies:
        copy.start()

    for part in range(2):
        cols = slice(part * 64, part * 64 + 64)
        for j in range(3):
            in_rows = slice(j * 256, j * 256 + 256)
            wqkv[:, part * 384 + j * 128 : part * 384 + j * 128 + 128] = jnp.concatenate(
                [own_ref[in_rows, cols], oth_ref[in_rows, cols]], 1
            )
        for pos, half in enumerate((own_ref, oth_ref)):
            dst_rows = slice(part * 128 + pos * 64, part * 128 + pos * 64 + 64)
            for col in range(2):
                natural = half[768 + 128 * col + part * 64 : 768 + 128 * col + part * 64 + 64, :]
                wout_t[dst_rows, col * 128 : col * 128 + 128] = natural
                turn = jnp.where(side == 0, col, 1 - col)
                start = pl.multiple_of(768 + 128 * turn + part * 64, 64)
                wout_p[dst_rows, col * 128 : col * 128 + 128] = half[pl.ds(start, 64), :]
    wout_t[...] = wout_t[...].T
    wq_own = wqkv[pl.ds(pl.multiple_of(side * 128, 128), 128), :]
    wq_oth = wqkv[pl.ds(pl.multiple_of((1 - side) * 128, 128), 128), :]
    wqkv_t[:, 0:128] = wq_own.T
    wqkv_t[:, 128:256] = wq_oth.T
    gacc[...] = jnp.zeros_like(gacc)
    gacc_o[...] = jnp.zeros_like(gacc_o)
    for copy in copies:
        copy.wait()

    row_iota = lax.broadcasted_iota(jnp.int32, (WINDOW, WINDOW), 0)

    def far_group(g, _):
        base = pl.multiple_of(g * GROUP, GROUP)
        x = xs[pl.ds(base, GROUP), :]
        for b in range(4):
            valid = lax.broadcasted_iota(jnp.int32, (WINDOW, 256), 0) < count_of(4 * g + b)
            piece = pl.ds(pl.multiple_of(base + b * WINDOW, WINDOW), WINDOW)
            cs[piece, :] = jnp.where(valid, cs[piece, :].astype(F32), 0.0).astype(BF)
        c = cs[pl.ds(base, GROUP), :]
        proj = mm(x, wqkv[...])
        dctx = mm(c, wout_t[...])
        near_in[pl.ds(base, GROUP), 0:384] = proj[:, 0:384].astype(BF)
        near_in[pl.ds(base, GROUP), 384:512] = dctx[:, 0:128].astype(BF)
        for j in range(3):
            far_stage[j] = proj[:, 384 + 128 * j : 512 + 128 * j]
        far_stage[3] = dctx[:, 128:256]
        loaded, masks = [], []
        for r in range(4):
            loaded.append([far_stage[j, pl.ds(r, WINDOW, stride=4), :].astype(BF) for j in range(4)])
            quarter = row_iota // 32
            limit = jnp.where(
                quarter < 2,
                jnp.where(quarter == 0, count_of(4 * g), count_of(4 * g + 1)),
                jnp.where(quarter == 2, count_of(4 * g + 2), count_of(4 * g + 3)),
            )
            masks.append(4 * (row_iota - 32 * quarter) + r < limit)
        for r, result in enumerate(windows_core(loaded, masks)):
            for j in range(4):
                far_res[j, pl.ds(r, WINDOW, stride=4), :] = result[j]
        for j in range(4):
            far_out[pl.ds(base, GROUP), 128 * j : 128 * j + 128] = far_res[j].astype(BF)
        return 0

    lax.fori_loop(0, ext // GROUP, far_group, 0)

    def near_windows(first, count):
        loaded, masks, places = [], [], []
        for i in range(count):
            w = first + i
            place = pl.ds(pl.multiple_of(192 + 128 * w, 64), WINDOW)
            block = near_in[place, :]
            loaded.append([block[:, 128 * j : 128 * j + 128] for j in range(4)])
            limit = jnp.where(row_iota < 64, count_of(w + 1) - 64, count_of(w + 2) + 64)
            masks.append(row_iota < limit)
            places.append(place)
        for place, result in zip(places, windows_core(loaded, masks)):
            for j in range(4):
                near_out[place, 128 * j : 128 * j + 128] = result[j].astype(BF)

    def near_step(s, _):
        near_windows(4 * s, 4)
        return 0

    total_near = rows // WINDOW + 1
    lax.fori_loop(0, total_near // 4, near_step, 0)
    if total_near % 4:
        near_windows(total_near // 4 * 4, total_near % 4)

    def finish(b, _):
        here = pl.ds(pl.multiple_of(HALO + GROUP * b, HALO), GROUP)
        there = pl.ds(pl.multiple_of(GROUP * b, GROUP), GROUP)
        near = near_out[here, :]
        far = far_out[here, :]
        ctx = jnp.concatenate([near[:, :128], far[:, :128]], 1)
        grads = jnp.concatenate([near[:, 128:], far[:, 128:]], 1)
        out = mm(ctx, wout_p[...])
        parts = []
        for q in range(4):
            valid = lax.broadcasted_iota(jnp.int32, (WINDOW, 256), 0) < count_of(4 * b + 2 + q)
            parts.append(jnp.where(valid, out[q * WINDOW : (q + 1) * WINDOW], 0.0))
        out = jnp.concatenate(parts, 0).astype(BF)
        out_keep[there, :] = out[:, :128]
        out_send[there, :] = out[:, 128:]
        gn = mm(grads, wqkv_t[...]).astype(BF)
        gn_keep[there, :] = gn[:, :128]
        gn_send[there, :] = gn[:, 128:]
        gacc[...] += mm(xs[here, :].T, grads)
        gacc_o[...] += mm(ctx.T, cs[here, :])
        return 0

    lax.fori_loop(0, rows // GROUP, finish, 0)

    for pos in range(2):
        half = side if pos == 0 else 1 - side
        for j in range(3):
            near = gacc[:, 128 * j + 64 * pos : 128 * j + 64 * pos + 64]
            far = gacc[:, 384 + 128 * j + 64 * pos : 384 + 128 * j + 64 * pos + 64]
            g_out[half, 256 * j : 256 * j + 256, :] = jnp.concatenate([near, far], 1) * norm
        for part in range(2):
            for col in range(2):
                piece = gacc_o[128 * part + 64 * pos : 128 * part + 64 * pos + 64, 128 * col : 128 * col + 128]
                low = 768 + 128 * col + 64 * part
                g_out[half, low : low + 64, :] = piece * norm
    if use_halo:
        g_out[...] = g_out[...] + g_in[...]


def local_call(rows, norm, meta, counts, nodes_in, cotangent, own, oth, halo=None, g_in=None):
    ext = rows + 2 * HALO
    use_halo = halo is not None
    vmem = pl.BlockSpec(memory_space=pltpu.VMEM)
    hbm = pl.BlockSpec(memory_space=pl.ANY)
    smem = pl.BlockSpec(memory_space=pltpu.SMEM)
    half = jax.ShapeDtypeStruct((rows, 128), BF)
    if use_halo:
        args = (meta, counts, nodes_in, cotangent, halo, own, oth, g_in)
        in_specs = [smem, smem, hbm, hbm, hbm, vmem, vmem, vmem]
    else:
        args = (meta, counts, nodes_in, cotangent, own, oth)
        in_specs = [smem, smem, hbm, hbm, vmem, vmem]

    def body(*refs):
        local_kernel(rows, use_halo, norm, *refs)

    return pl.pallas_call(
        body,
        out_shape=(half, half, half, half, jax.ShapeDtypeStruct((2, 1024, 128), F32)),
        in_specs=in_specs,
        out_specs=(vmem,) * 5,
        scratch_shapes=[
            pltpu.VMEM((ext, 256), BF),
            pltpu.VMEM((ext, 256), BF),
            pltpu.VMEM((ext, 512), BF),
            pltpu.VMEM((ext, 512), BF),
            pltpu.VMEM((ext, 512), BF),
            pltpu.VMEM((4, GROUP, 128), F32),
            pltpu.VMEM((4, GROUP, 128), F32),
            pltpu.VMEM((256, 768), BF),
            pltpu.VMEM((768, 256), BF),
            pltpu.VMEM((256, 256), BF),
            pltpu.VMEM((256, 256), BF),
            pltpu.VMEM((256, 768), F32),
            pltpu.VMEM((256, 256), F32),
            pltpu.SemaphoreType.DMA((4,)),
        ],
        compiler_params=pltpu.CompilerParams(vmem_limit_bytes=56 * 1024 * 1024),
        cost_estimate=pl.CostEstimate(flops=rows * 4000000, bytes_accessed=rows * 3000, transcendentals=0),
    )(*args)


def per_device(nodes_in, cotangent, w_query, w_key, w_value, w_out, counts):
    row_count = nodes_in.shape[0]
    quarter = row_count // 4
    side = lax.axis_index("head").astype(jnp.int32)
    place = lax.axis_index(("gz", "tile")).astype(jnp.int32)
    gz, heads, tiles = lax.axis_size("gz"), lax.axis_size("head"), lax.axis_size("tile")
    places = gz * tiles
    swap = [(0, 1), (1, 0)]

    own = jnp.concatenate([w_query, w_key, w_value, w_out[:, :128], w_out[:, 128:]], 0)
    oth = lax.ppermute(own, "head", swap)

    def flat(p, h):
        return (p // tiles * heads + h) * tiles + p % tiles

    rim = (1 - side) * (row_count - HALO)
    rims = jnp.concatenate(
        [lax.dynamic_slice_in_dim(nodes_in, rim, HALO), lax.dynamic_slice_in_dim(cotangent, rim, HALO)], 1
    )
    route = [(flat(p, 0), flat((p + 1) % places, 0)) for p in range(places)]
    route += [(flat(p, 1), flat((p - 1) % places, 1)) for p in range(places)]
    halo = lax.ppermute(rims, ("gz", "head", "tile"), route)

    norm = float(row_count * places) ** (-0.5)
    blocks = row_count // WINDOW

    def meta_of(first_row, source):
        first_block = (place * blocks + counts.shape[0] + (first_row - HALO) // WINDOW) % counts.shape[0]
        return jnp.stack([first_block, side, source]).astype(jnp.int32)

    row_a = quarter * (1 + side)
    row_b = 3 * quarter * side
    a = local_call(quarter, norm, meta_of(row_a, row_a - HALO), counts, nodes_in, cotangent, own, oth)
    sent_a = [lax.ppermute(a[1], "head", swap), lax.ppermute(a[3], "head", swap)]
    source_b = side * (row_b - HALO)
    b = local_call(
        quarter, norm, meta_of(row_b, source_b), counts, nodes_in, cotangent, own, oth, halo, a[4]
    )
    sent_b = [lax.ppermute(b[1], "head", swap), lax.ppermute(b[3], "head", swap)]

    grads = b[4].reshape(heads * places, 1024 // places, 128)
    grads = lax.all_to_all(grads, ("head", "gz", "tile"), 0, 0, tiled=True)
    share = jnp.sum(grads, axis=0)
    share = jnp.broadcast_to(share[None], (places,) + share.shape)
    whole = lax.all_to_all(share, ("gz", "tile"), 0, 0, tiled=True).reshape(1024, 128)

    other_a = quarter * (2 - side)
    other_b = 3 * quarter * (1 - side)

    def assemble(keep_a, keep_b, got_a, got_b):
        full = jnp.zeros((row_count, 128), BF)
        for rows, first in ((keep_a, row_a), (keep_b, row_b), (got_a, other_a), (got_b, other_b)):
            full = lax.dynamic_update_slice(full, rows, (first, 0))
        return full

    output = assemble(a[0], b[0], sent_a[0], sent_b[0])
    grad_nodes = assemble(a[2], b[2], sent_a[1], sent_b[1])
    grad_out = jnp.concatenate([whole[768:896], whole[896:1024]], 1)
    return (output, grad_nodes, whole[0:256], whole[256:512], whole[512:768], grad_out)


def solution(mesh):
    return jax.shard_map(
        per_device,
        mesh=mesh,
        in_specs=(
            P(("gz", "tile"), None),
            P(("gz", "tile"), None),
            P(None, "head"),
            P(None, "head"),
            P(None, "head"),
            P("head", None),
            P(),
        ),
        out_specs=(
            P(("gz", "tile"), "head"),
            P(("gz", "tile"), "head"),
            P(None, "head"),
            P(None, "head"),
            P(None, "head"),
            P("head", None),
        ),
        check_vma=False,
    )
```

```python
import functools
import math

import jax
import jax.numpy as jnp
from jax import lax
from jax.experimental import pallas as pl
from jax.experimental.pallas import tpu as pltpu
from jax.sharding import PartitionSpec as P

WINDOW = 128
HALO = 256
GROUP = 512
HEAD_DIM = 32
CALL_GROUPS = (3, 3, 3)
BEYOND = 3
SCALE = HEAD_DIM ** (-0.5)
EXP2_SCALE = SCALE * math.log2(math.e)
VMEM_LIMIT = 56 * 1024 * 1024
BF = jnp.bfloat16
F32 = jnp.float32


def mm(a, b):
    return jnp.dot(a, b, preferred_element_type=F32)


def mm_nt(a, b):
    return lax.dot_general(a, b, (((1,), (1,)), ((), ())), preferred_element_type=F32)


def head_masks():
    lane_head = lax.broadcasted_iota(jnp.int32, (WINDOW, WINDOW), 1) // HEAD_DIM
    return [jnp.where(lane_head == h, 1.0, 0.0).astype(BF) for h in range(4)]


class Window:
    def __init__(self, load, mask, store, spread):
        self.load, self.mask, self.store, self.spread = load, mask, store, spread

    def scores(self):
        q, k, v, d = self.load()
        self.keep = self.mask().astype(F32)
        self.q4 = jnp.concatenate([q * m for m in self.spread], 0)
        self.d4 = jnp.concatenate([d * m for m in self.spread], 0)
        self.s = mm_nt(k, self.q4)
        self.da = mm_nt(v, self.d4)
        self.k_t, self.v_t = k.T, v.T

    def softmax(self):
        low, dsc = [], []
        for h in range(4):
            cols = slice(h * WINDOW, (h + 1) * WINDOW)
            e = jnp.exp2(self.s[:, cols] * EXP2_SCALE) * self.keep
            a = e * (1.0 / jnp.sum(e, axis=0, keepdims=True))
            d = self.da[:, cols]
            center = jnp.sum(a * d, axis=0, keepdims=True)
            low.append(a.astype(BF))
            dsc.append((a * (d - center)).astype(BF))
        self.low = jnp.concatenate(low, 1)
        self.dsc = jnp.concatenate(dsc, 1)

    def outputs(self):
        ctx_t, dq_t = [], []
        for pair in range(2):
            rows = slice(pair * 64, pair * 64 + 64)
            cols = slice(pair * 256, pair * 256 + 256)
            c2 = mm(self.v_t[rows], self.low[:, cols])
            q2 = mm(self.k_t[rows], self.dsc[:, cols])
            ctx_t += [c2[:32, :128], c2[32:, 128:]]
            dq_t += [q2[:32, :128], q2[32:, 128:]]
        dv = mm(self.low, self.d4)
        dk = mm(self.dsc, self.q4) * SCALE
        ctx = jnp.concatenate(ctx_t, 0).T
        dq = jnp.concatenate(dq_t, 0).T * SCALE
        self.store((ctx, dq, dk, dv))


def build_weights(side, own_ref, oth_ref, wqkv, wqkv_t, wout_t, wout_p):
    for part in range(2):
        cols = slice(part * 64, part * 64 + 64)
        for j in range(3):
            in_rows = slice(j * 256, j * 256 + 256)
            wqkv[:, part * 384 + j * 128 : part * 384 + j * 128 + 128] = jnp.concatenate(
                [own_ref[in_rows, cols], oth_ref[in_rows, cols]], 1
            )
        for pos, half in enumerate((own_ref, oth_ref)):
            dst_rows = slice(part * 128 + pos * 64, part * 128 + pos * 64 + 64)
            for col in range(2):
                natural = half[768 + 128 * col + part * 64 : 768 + 128 * col + part * 64 + 64, :]
                wout_t[dst_rows, col * 128 : col * 128 + 128] = natural
                turn = jnp.where(side == 0, col, 1 - col)
                start = pl.multiple_of(768 + 128 * turn + part * 64, 64)
                wout_p[dst_rows, col * 128 : col * 128 + 128] = half[pl.ds(start, 64), :]
    wout_t[...] = wout_t[...].T
    wqkv_t[:, 0:128] = wqkv[pl.ds(pl.multiple_of(side * 128, 128), 128), :].T
    wqkv_t[:, 128:256] = wqkv[pl.ds(pl.multiple_of((1 - side) * 128, 128), 128), :].T


class Plan:
    def __init__(self, first_group, groups, first, last, beyond, send, got):
        self.first_group, self.groups = first_group, groups
        self.first, self.last, self.beyond, self.send = first, last, beyond, send
        self.got = got
        self.blocks = groups - (1 if first else 0)
        self.rows = self.blocks * GROUP


def chunk_kernel(plan, norm, *refs):
    refs = list(refs)
    take = lambda n: [refs.pop(0) for _ in range(n)]
    groups, first = plan.groups, plan.first
    grads_on = not plan.beyond
    counts_hbm, x_hbm, c_hbm = take(3)
    if first:
        halo_hbm, own_ref, oth_ref = take(3)
    else:
        weights_c = take(4)
        carry_c = take(3)
        gacc_c = take(1)[0] if grads_on else None
        take(2)
    got_hbm = take(1)[0] if plan.got else None
    out_full, gn_full = take(2)
    send = take(1)[0] if plan.send else None
    if first:
        weights = take(4)
    carry_n = take(3) if grads_on else None
    g_out = take(1)[0] if grads_on else None
    (xs, cs, near_in, near_out, far_out, far_stage, far_res, gacc, gacc_in, keep_o, keep_g, send_st, counts) = take(13)
    in_sems, misc_sems, out_sems = take(3)
    if not first:
        weights = take(4)
    if plan.got:
        got_st, got_sems = take(2)
    wqkv, wqkv_t, wout_t, wout_p = weights

    side = lax.axis_index("head").astype(jnp.int32)
    place = lax.axis_index(("gz", "tile")).astype(jnp.int32)
    total_blocks = counts.shape[0]
    slab = x_hbm.shape[0]
    width = xs.shape[1]
    up = GROUP * plan.first_group - GROUP
    down = slab - HALO - GROUP * (plan.first_group + groups - 1)
    origin = up + side * (down - up)
    first_block = place * (slab // WINDOW) + (origin + GROUP) // WINDOW - GROUP // WINDOW + total_blocks
    carry_in = pl.ds(pl.multiple_of(side * groups * GROUP, HALO), HALO)
    carry_out = pl.ds(pl.multiple_of((1 - side) * groups * GROUP, HALO), HALO)

    def count_of(row):
        return counts[lax.rem(first_block + row // WINDOW, total_blocks)]

    def piece_place(k):
        piece = k + side * (2 * groups - 2 * k)
        return piece, pl.ds(pl.multiple_of(piece * HALO, HALO), HALO)

    copies = [pltpu.make_async_copy(counts_hbm, counts, misc_sems.at[0])]
    if not first:
        for k in range(4):
            copies.append(pltpu.make_async_copy(weights_c[k], weights[k], misc_sems.at[1 + k]))
        for k, buffer in enumerate((near_in, near_out, far_out)):
            copies.append(pltpu.make_async_copy(carry_c[k], buffer.at[carry_in], misc_sems.at[5 + k]))
    for copy in copies:
        copy.start()
    for k in range(1 if first else 0, 2 * groups + 1):
        piece, dst = piece_place(k)
        if first and k == 1:
            pltpu.make_async_copy(halo_hbm.at[:, pl.ds(0, width)], xs.at[dst], in_sems.at[k, 0]).start()
            pltpu.make_async_copy(halo_hbm.at[:, pl.ds(width, width)], cs.at[dst], in_sems.at[k, 1]).start()
        else:
            src = pl.ds(pl.multiple_of(origin + piece * HALO, HALO), HALO)
            pltpu.make_async_copy(x_hbm.at[src], xs.at[dst], in_sems.at[k, 0]).start()
            pltpu.make_async_copy(c_hbm.at[src], cs.at[dst], in_sems.at[k, 1]).start()
    if plan.got:
        got_load = pltpu.make_async_copy(got_hbm, got_st, got_sems.at[2])
        got_load.start()
    if grads_on and not first:
        gacc_load = pltpu.make_async_copy(gacc_c, gacc_in, misc_sems.at[8])
        gacc_load.start()

    def wait_piece(k):
        _, dst = piece_place(k)
        pltpu.make_async_copy(x_hbm.at[pl.ds(0, HALO)], xs.at[dst], in_sems.at[k, 0]).wait()
        pltpu.make_async_copy(c_hbm.at[pl.ds(0, HALO)], cs.at[dst], in_sems.at[k, 1]).wait()

    row_iota = lax.broadcasted_iota(jnp.int32, (WINDOW, WINDOW), 0)
    wide_iota = lax.broadcasted_iota(jnp.int32, (WINDOW, 256), 0)

    def mask_cot(start):
        piece = pl.ds(pl.multiple_of(start, WINDOW), WINDOW)
        cs[piece, :] = jnp.where(wide_iota < count_of(start), cs[piece, :].astype(F32), 0.0).astype(BF)

    if first:
        build_weights(side, own_ref, oth_ref, wqkv, wqkv_t, wout_t, wout_p)
    if grads_on:
        gacc[...] = jnp.zeros_like(gacc)
    for copy in copies:
        copy.wait()
    if not first:
        wait_piece(0)
        for b in range(2):
            mask_cot(side * groups * GROUP + b * WINDOW)

    def base_of(i):
        return HALO + i * GROUP + side * (GROUP * groups - 3 * HALO - 2 * GROUP * i)

    def ready_of(base, part):
        return base - HALO + part * HALO + side * (3 * HALO - 2 * HALO * part)

    def result_copies(i):
        start = pl.multiple_of(ready_of(base_of(i), 0) - side * HALO, HALO)
        here = pl.ds(start, GROUP)
        final = pl.ds(pl.multiple_of(origin + start, HALO), GROUP)
        found = [
            pltpu.make_async_copy(keep_o.at[here], out_full.at[final], out_sems.at[i, 0]),
            pltpu.make_async_copy(keep_g.at[here], gn_full.at[final], out_sems.at[i, 1]),
        ]
        if plan.send:
            first_row = (1 - side) * (GROUP if first else 0) + side * HALO
            there = pl.ds(pl.multiple_of(start - first_row, HALO), GROUP)
            found.append(pltpu.make_async_copy(send_st.at[here], send.at[there], out_sems.at[i, 2]))
        return found

    def step(i, with_finish):
        base = pl.multiple_of(base_of(i), HALO)
        here = pl.ds(base, GROUP)
        wait_piece(2 * i + 1)
        wait_piece(2 * i + 2)
        for b in range(4):
            mask_cot(base + b * WINDOW)
        proj = mm(xs[here, :], wqkv[...])
        dctx = mm(cs[here, :], wout_t[...])
        near_in[here, 0:384] = proj[:, 0:384].astype(BF)
        near_in[here, 384:512] = dctx[:, 0:128].astype(BF)
        for j in range(3):
            far_stage[j] = proj[:, 384 + 128 * j : 512 + 128 * j]
        far_stage[3] = dctx[:, 128:256]
        spread = head_masks()

        def far_window(r):
            def load():
                return [far_stage[j, pl.ds(r, WINDOW, stride=4), :].astype(BF) for j in range(4)]

            def mask():
                quarter = row_iota // 32
                limit = jnp.where(
                    quarter < 2,
                    jnp.where(quarter == 0, count_of(base), count_of(base + WINDOW)),
                    jnp.where(quarter == 2, count_of(base + 2 * WINDOW), count_of(base + 3 * WINDOW)),
                )
                return 4 * (row_iota - 32 * quarter) + r < limit

            def store(result):
                for j in range(4):
                    far_res[j, pl.ds(r, WINDOW, stride=4), :] = result[j]

            return Window(load, mask, store, spread)

        def near_window(k):
            start = base - 64 + WINDOW * k + side * (WINDOW + WINDOW * (3 - 2 * k))
            spot = pl.ds(pl.multiple_of(start, 64), WINDOW)

            def load():
                block = near_in[spot, :]
                return [block[:, 128 * j : 128 * j + 128] for j in range(4)]

            def mask():
                limit = jnp.where(row_iota < 64, count_of(start - 64) - 64, count_of(start + 64) + 64)
                return row_iota < limit

            def store(result):
                for j in range(4):
                    near_out[spot, 128 * j : 128 * j + 128] = result[j].astype(BF)

            return Window(load, mask, store, spread)

        def finish(part):
            start = pl.multiple_of(ready_of(base, part), HALO)
            ready = pl.ds(start, HALO)
            near = near_out[ready, :]
            far = far_out[ready, :]
            ctx = jnp.concatenate([near[:, :128], far[:, :128]], 1)
            grads = jnp.concatenate([near[:, 128:], far[:, 128:]], 1)
            wp, wt = (wout_p, wqkv_t) if plan.send else (wout_p.at[:, pl.ds(0, 128)], wqkv_t.at[:, pl.ds(0, 128)])
            out = mm(ctx, wp[...])
            parts = []
            for q in range(2):
                rows = slice(q * WINDOW, (q + 1) * WINDOW)
                keep = wide_iota[:, : out.shape[1]] < count_of(start + q * WINDOW)
                parts.append(jnp.where(keep, out[rows], 0.0))
            out = jnp.concatenate(parts, 0).astype(BF)
            gn = mm(grads, wt[...]).astype(BF)
            keep_o[ready, :] = out[:, :128]
            keep_g[ready, :] = gn[:, :128]
            if plan.send:
                send_st[ready, 0:128] = out[:, 128:]
                send_st[ready, 128:256] = gn[:, 128:]
            if grads_on:
                gacc[:, 0:768] += mm(turned_x[part], grads)
                gacc[:, 768:1024] += mm(turned_c[part], ctx)

        if with_finish and grads_on:
            halves = [pl.ds(pl.multiple_of(ready_of(base, p), HALO), HALO) for p in range(2)]
            turned_x = [xs[half, :].T for half in halves]
            turned_c = [cs[half, :].T for half in halves]

        line = [near_window(0)] + [far_window(r) for r in range(4)] + [near_window(k) for k in range(1, 4)]
        count = len(line)
        for t in range(count + 2):
            if t < count:
                line[t].scores()
            if 1 <= t <= count:
                line[t - 1].softmax()
            if t >= 2:
                line[t - 2].outputs()
            if t == 3 and with_finish:
                finish(0)
            if t == 6:
                for j in range(4):
                    far_out[here, 128 * j : 128 * j + 128] = far_res[j].astype(BF)
        if with_finish:
            finish(1)
            for copy in result_copies(i):
                copy.start()

    start = 0
    if first:
        step(0, False)
        start = 1
    if plan.got:
        got_load.wait()
        row, size = plan.got
        theirs = side * row + (1 - side) * (slab - row - size)
        theirs = pl.ds(pl.multiple_of(theirs, HALO), size)
        got_copies = (
            pltpu.make_async_copy(got_st.at[:, pl.ds(0, 128)], out_full.at[theirs], got_sems.at[0]),
            pltpu.make_async_copy(got_st.at[:, pl.ds(128, 128)], gn_full.at[theirs], got_sems.at[1]),
        )
        for copy in got_copies:
            copy.start()

    def loop_body(i, _):
        step(i, True)
        return 0

    lax.fori_loop(start, groups, loop_body, 0)

    if grads_on:
        passed = [
            pltpu.make_async_copy(near_in.at[carry_out], carry_n[0], misc_sems.at[0]),
            pltpu.make_async_copy(near_out.at[carry_out], carry_n[1], misc_sems.at[1]),
            pltpu.make_async_copy(far_out.at[carry_out], carry_n[2], misc_sems.at[2]),
        ]
        for copy in passed:
            copy.start()
        if not first:
            gacc_load.wait()
            gacc[...] = gacc[...] + gacc_in[...]
        if plan.last:
            turned_out = gacc[:, 768:1024].T
            for pos in range(2):
                half = side if pos == 0 else 1 - side
                for j in range(3):
                    near = gacc[:, 128 * j + 64 * pos : 128 * j + 64 * pos + 64]
                    far = gacc[:, 384 + 128 * j + 64 * pos : 384 + 128 * j + 64 * pos + 64]
                    g_out[half, 256 * j : 256 * j + 256, :] = (jnp.concatenate([near, far], 1) * norm).astype(BF)
                for part in range(2):
                    for col in range(2):
                        rows = slice(128 * part + 64 * pos, 128 * part + 64 * pos + 64)
                        piece = turned_out[rows, 128 * col : 128 * col + 128]
                        low = 768 + 128 * col + 64 * part
                        g_out[half, low : low + 64, :] = (piece * norm).astype(BF)
        else:
            passed.append(pltpu.make_async_copy(gacc, g_out, misc_sems.at[3]))
            passed[-1].start()
        for copy in passed:
            copy.wait()
    for i in range(1 if first else 0, groups):
        for copy in result_copies(i):
            copy.wait()
    if plan.got:
        for copy in got_copies:
            copy.wait()


def chunk_call(plan, norm, counts, nodes_in, cotangent, halo, weights, carry, gacc, fulls, got):
    vmem = pl.BlockSpec(memory_space=pltpu.VMEM)
    hbm = pl.BlockSpec(memory_space=pl.ANY)
    slab = nodes_in.shape[0]
    groups, first, grads_on = plan.groups, plan.first, not plan.beyond
    buffer = HALO + groups * GROUP
    sds = jax.ShapeDtypeStruct
    weight_shapes = [(256, 768), (768, 256), (256, 256), (256, 256)]
    aliases = {}
    if first:
        args = [counts, nodes_in, cotangent, halo] + list(weights)
        in_specs = [hbm] * 4 + [vmem] * 2
    else:
        args = [counts, nodes_in, cotangent] + list(weights) + list(carry) + ([gacc] if grads_on else []) + list(fulls)
        in_specs = [hbm] * len(args)
        aliases = {len(args) - 2: 0, len(args) - 1: 1}
    if got is not None:
        args.append(got)
        in_specs.append(hbm)
    out_shape = [sds((slab, 128), BF), sds((slab, 128), BF)]
    if plan.send:
        out_shape.append(sds((plan.rows, 256), BF))
    out_specs = [hbm] * len(out_shape)
    if first:
        out_shape += [sds(shape, BF) for shape in weight_shapes]
        out_specs += [vmem] * 4
    if grads_on:
        out_shape += [sds((HALO, 512), BF)] * 3
        out_specs += [hbm] * 3
        out_shape.append(sds((2, 1024, 128), BF) if plan.last else sds((256, 1024), F32))
        out_specs.append(vmem if plan.last else hbm)
    scratch = [
        pltpu.VMEM((buffer, 256), BF),
        pltpu.VMEM((buffer, 256), BF),
        pltpu.VMEM((buffer, 512), BF),
        pltpu.VMEM((buffer, 512), BF),
        pltpu.VMEM((buffer, 512), BF),
        pltpu.VMEM((4, GROUP, 128), F32),
        pltpu.VMEM((4, GROUP, 128), F32),
        pltpu.VMEM((256, 1024), F32),
        pltpu.VMEM((256, 1024), F32),
        pltpu.VMEM((buffer, 128), BF),
        pltpu.VMEM((buffer, 128), BF),
        pltpu.VMEM((buffer, 256), BF),
        pltpu.SMEM((counts.shape[0],), jnp.int32),
        pltpu.SemaphoreType.DMA((2 * groups + 1, 2)),
        pltpu.SemaphoreType.DMA((9,)),
        pltpu.SemaphoreType.DMA((groups, 3)),
    ]
    if not first:
        scratch += [pltpu.VMEM(shape, BF) for shape in weight_shapes]
    if got is not None:
        scratch += [pltpu.VMEM(got.shape, BF), pltpu.SemaphoreType.DMA((3,))]
    outs = pl.pallas_call(
        functools.partial(chunk_kernel, plan, norm),
        out_shape=out_shape,
        in_specs=in_specs,
        out_specs=out_specs,
        input_output_aliases=aliases,
        scratch_shapes=scratch,
        compiler_params=pltpu.CompilerParams(vmem_limit_bytes=VMEM_LIMIT),
        cost_estimate=pl.CostEstimate(
            flops=plan.rows * 4000000, bytes_accessed=plan.rows * 3000, transcendentals=0
        ),
    )(*args)
    outs = list(outs)
    fulls, rest = outs[:2], outs[2:]
    sent = rest.pop(0) if plan.send else None
    if first:
        weights, rest = rest[:4], rest[4:]
    if grads_on:
        carry, gacc = rest[:3], rest[3]
    return fulls, sent, weights, carry, gacc


def pack_kernel(x_hbm, c_hbm, wq, wk, wv, wo, packed, rims, sems):
    side = lax.axis_index("head").astype(jnp.int32)
    rows = pl.ds(pl.multiple_of((1 - side) * (x_hbm.shape[0] - HALO), HALO), HALO)
    copies = (
        pltpu.make_async_copy(x_hbm.at[rows], rims.at[:, pl.ds(0, 256)], sems.at[0]),
        pltpu.make_async_copy(c_hbm.at[rows], rims.at[:, pl.ds(256, 256)], sems.at[1]),
    )
    for copy in copies:
        copy.start()
    packed[0:256, :] = wq[...]
    packed[256:512, :] = wk[...]
    packed[512:768, :] = wv[...]
    packed[768:896, :] = wo[:, 0:128]
    packed[896:1024, :] = wo[:, 128:256]
    for copy in copies:
        copy.wait()


def pack_call(nodes_in, cotangent, w_query, w_key, w_value, w_out):
    vmem = pl.BlockSpec(memory_space=pltpu.VMEM)
    hbm = pl.BlockSpec(memory_space=pl.ANY)
    return pl.pallas_call(
        pack_kernel,
        out_shape=(jax.ShapeDtypeStruct((1024, 128), BF), jax.ShapeDtypeStruct((HALO, 512), BF)),
        in_specs=[hbm, hbm, vmem, vmem, vmem, vmem],
        out_specs=(vmem, vmem),
        scratch_shapes=[pltpu.SemaphoreType.DMA((2,))],
    )(nodes_in, cotangent, w_query, w_key, w_value, w_out)


def per_device(nodes_in, cotangent, w_query, w_key, w_value, w_out, counts):
    row_count = nodes_in.shape[0]
    gz, heads, tiles = lax.axis_size("gz"), lax.axis_size("head"), lax.axis_size("tile")
    places = gz * tiles
    swap = [(0, 1), (1, 0)]

    def flat(p, h):
        return (p // tiles * heads + h) * tiles + p % tiles

    own, rims = pack_call(nodes_in, cotangent, w_query, w_key, w_value, w_out)
    oth = lax.ppermute(own, "head", swap)
    route = [(flat(p, 0), flat((p + 1) % places, 0)) for p in range(places)]
    route += [(flat(p, 1), flat((p - 1) % places, 1)) for p in range(places)]
    halo = lax.ppermute(rims, ("gz", "head", "tile"), route)

    norm = float(row_count * places) ** (-0.5)
    weights, carry, gacc, fulls = (own, oth), None, None, None
    waiting, first_group, row = [], 0, 0
    for n, groups in enumerate(CALL_GROUPS + (BEYOND,)):
        first, beyond = n == 0, n == len(CALL_GROUPS)
        last = n == len(CALL_GROUPS) - 1
        send = not last and not beyond
        got_rows, got = waiting.pop(0) if len(waiting) > (0 if beyond else 1) else (None, None)
        spot = None if got is None else (got_rows, got.shape[0])
        plan = Plan(first_group, groups, first, last, beyond, send, spot)
        fulls, sent, weights, carry, gacc = chunk_call(
            plan, norm, counts, nodes_in, cotangent, halo, weights, carry, gacc, fulls, got
        )
        if send:
            waiting.append((row, lax.ppermute(sent, "head", swap)))
        first_group += groups
        row += plan.rows

    part = 1024 // places
    grads = gacc.reshape(heads * places, part, 128)
    grads = lax.all_to_all(grads, ("head", "gz", "tile"), 0, 0, tiled=True)
    share = jnp.sum(grads.astype(F32), axis=0).astype(BF)
    share, *fulls = lax.optimization_barrier((share, *fulls))
    share = jnp.broadcast_to(share[None], (places,) + share.shape)
    whole = lax.all_to_all(share, ("gz", "tile"), 0, 0, tiled=True).reshape(1024, 128).astype(F32)
    grad_out = jnp.concatenate([whole[768:896], whole[896:1024]], 1)
    return (fulls[0], fulls[1], whole[0:256], whole[256:512], whole[512:768], grad_out)


def solution(mesh):
    return jax.shard_map(
        per_device,
        mesh=mesh,
        in_specs=(
            P(("gz", "tile"), None),
            P(("gz", "tile"), None),
            P(None, "head"),
            P(None, "head"),
            P(None, "head"),
            P("head", None),
            P(),
        ),
        out_specs=(
            P(("gz", "tile"), "head"),
            P(("gz", "tile"), "head"),
            P(None, "head"),
            P(None, "head"),
            P(None, "head"),
            P("head", None),
        ),
        check_vma=False,
    )
```

```python
import functools
import math

import jax
import jax.numpy as jnp
from jax import lax
from jax.experimental import pallas as pl
from jax.experimental.pallas import tpu as pltpu
from jax.sharding import PartitionSpec as P

WINDOW = 128
HALO = 256
GROUP = 512
HEAD_DIM = 32
OWN_CALLS = (4, 5)
BEYOND_CALLS = (3, 2)
SCALE = HEAD_DIM ** (-0.5)
EXP2_SCALE = SCALE * math.log2(math.e)
VMEM_LIMIT = 58 * 1024 * 1024
BF = jnp.bfloat16
F32 = jnp.float32


def mm(a, b):
    return jnp.dot(a, b, preferred_element_type=F32)


def mm_nt(a, b):
    return lax.dot_general(a, b, (((1,), (1,)), ((), ())), preferred_element_type=F32)


def head_masks():
    lane_head = lax.broadcasted_iota(jnp.int32, (WINDOW, WINDOW), 1) // HEAD_DIM
    return [jnp.where(lane_head == h, 1.0, 0.0).astype(BF) for h in range(4)]


class Window:
    def __init__(self, load, mask, store, spread):
        self.load, self.mask, self.store, self.spread = load, mask, store, spread

    def scores(self):
        q, k, v, d = self.load()
        self.keep = self.mask().astype(F32)
        self.q4 = jnp.concatenate([q * m for m in self.spread], 0)
        self.d4 = jnp.concatenate([d * m for m in self.spread], 0)
        self.s = mm_nt(k, self.q4)
        self.da = mm_nt(v, self.d4)
        self.k_t, self.v_t = k.T, v.T

    def softmax(self):
        low, dsc = [], []
        for h in range(4):
            cols = slice(h * WINDOW, (h + 1) * WINDOW)
            e = jnp.exp2(self.s[:, cols] * EXP2_SCALE) * self.keep
            a = e * (1.0 / jnp.sum(e, axis=0, keepdims=True))
            d = self.da[:, cols]
            center = jnp.sum(a * d, axis=0, keepdims=True)
            low.append(a.astype(BF))
            dsc.append((a * (d - center)).astype(BF))
        self.low = jnp.concatenate(low, 1)
        self.dsc = jnp.concatenate(dsc, 1)

    def outputs(self):
        ctx_t, dq_t = [], []
        for pair in range(2):
            rows = slice(pair * 64, pair * 64 + 64)
            cols = slice(pair * 256, pair * 256 + 256)
            c2 = mm(self.v_t[rows], self.low[:, cols])
            q2 = mm(self.k_t[rows], self.dsc[:, cols])
            ctx_t += [c2[:32, :128], c2[32:, 128:]]
            dq_t += [q2[:32, :128], q2[32:, 128:]]
        dv = mm(self.low, self.d4)
        dk = mm(self.dsc, self.q4) * SCALE
        ctx = jnp.concatenate(ctx_t, 0).T
        dq = jnp.concatenate(dq_t, 0).T * SCALE
        self.store((ctx, dq, dk, dv))


def build_weights(side, own_ref, oth_ref, wqkv, wqkv_t, wout_t, wout_p):
    for part in range(2):
        cols = slice(part * 64, part * 64 + 64)
        for j in range(3):
            in_rows = slice(j * 256, j * 256 + 256)
            wqkv[:, part * 384 + j * 128 : part * 384 + j * 128 + 128] = jnp.concatenate(
                [own_ref[in_rows, cols], oth_ref[in_rows, cols]], 1
            )
        for pos, half in enumerate((own_ref, oth_ref)):
            dst_rows = slice(part * 128 + pos * 64, part * 128 + pos * 64 + 64)
            for col in range(2):
                natural = half[768 + 128 * col + part * 64 : 768 + 128 * col + part * 64 + 64, :]
                wout_t[dst_rows, col * 128 : col * 128 + 128] = natural
                turn = jnp.where(side == 0, col, 1 - col)
                start = pl.multiple_of(768 + 128 * turn + part * 64, 64)
                wout_p[dst_rows, col * 128 : col * 128 + 128] = half[pl.ds(start, 64), :]
    wout_t[...] = wout_t[...].T
    wqkv_t[:, 0:128] = wqkv[pl.ds(pl.multiple_of(side * 128, 128), 128), :].T
    wqkv_t[:, 128:256] = wqkv[pl.ds(pl.multiple_of((1 - side) * 128, 128), 128), :].T


class Plan:
    def __init__(self, first_group, groups, first, last, beyond, send, carry, got):
        self.first_group, self.groups = first_group, groups
        self.first, self.last, self.beyond, self.send = first, last, beyond, send
        self.carry = carry
        self.got = got
        self.blocks = groups - (1 if first else 0)
        self.cost = 200000 if beyond else 4000000
        self.rows = self.blocks * GROUP


def chunk_kernel(plan, norm, *refs):
    refs = list(refs)
    take = lambda n: [refs.pop(0) for _ in range(n)]
    groups, first = plan.groups, plan.first
    grads_on = not plan.beyond
    counts_hbm, x_hbm, c_hbm = take(3)
    if first:
        halo_hbm, own_hbm, oth_hbm = take(3)
    else:
        weights_c = take(4)
        carry_c = take(3)
        gacc_c = take(1)[0] if grads_on else None
        take(2)
    got_hbm = take(1)[0] if plan.got else None
    out_full, gn_full = take(2)
    send = take(1)[0] if plan.send else None
    if first:
        weights = take(4)
    carry_n = take(3) if plan.carry else None
    g_out = take(1)[0] if grads_on else None
    (xs, cs, near_in, near_out, far_out, far_stage, far_res, gacc, gacc_in, keep_o, keep_g, send_st, counts) = take(13)
    in_sems, misc_sems, out_sems = take(3)
    if first:
        own_ref, oth_ref = take(2)
    else:
        weights = take(4)
    if plan.got:
        got_st, got_sems = take(2)
    wqkv, wqkv_t, wout_t, wout_p = weights

    side = lax.axis_index("head").astype(jnp.int32)
    place = lax.axis_index(("gz", "tile")).astype(jnp.int32)
    total_blocks = counts.shape[0]
    slab = x_hbm.shape[0]
    up = GROUP * plan.first_group - GROUP
    down = slab - HALO - GROUP * (plan.first_group + groups - 1)
    origin = up + side * (down - up)
    first_block = place * (slab // WINDOW) + (origin + GROUP) // WINDOW - GROUP // WINDOW + total_blocks
    carry_in = pl.ds(pl.multiple_of(side * groups * GROUP, HALO), HALO)
    carry_out = pl.ds(pl.multiple_of((1 - side) * groups * GROUP, HALO), HALO)

    def count_of(row):
        return counts[lax.rem(first_block + row // WINDOW, total_blocks)]

    def piece_place(k):
        piece = k + side * (2 * groups - 2 * k)
        return piece, pl.ds(pl.multiple_of(piece * HALO, HALO), HALO)

    copies = [pltpu.make_async_copy(counts_hbm, counts, misc_sems.at[0])]
    if first:
        copies.append(pltpu.make_async_copy(own_hbm, own_ref, misc_sems.at[1]))
        copies.append(pltpu.make_async_copy(oth_hbm, oth_ref, misc_sems.at[2]))
    else:
        for k in range(4):
            copies.append(pltpu.make_async_copy(weights_c[k], weights[k], misc_sems.at[1 + k]))
        for k, buffer in enumerate((near_in, near_out, far_out)):
            copies.append(pltpu.make_async_copy(carry_c[k], buffer.at[carry_in], misc_sems.at[5 + k]))
    for copy in copies:
        copy.start()
    for k in range(1 if first else 0, 2 * groups + 1):
        piece, dst = piece_place(k)
        if first and k == 1:
            pltpu.make_async_copy(halo_hbm.at[:, pl.ds(0, 256)], xs.at[dst], in_sems.at[k, 0]).start()
            pltpu.make_async_copy(halo_hbm.at[:, pl.ds(256, 256)], cs.at[dst], in_sems.at[k, 1]).start()
        else:
            src = pl.ds(pl.multiple_of(origin + piece * HALO, HALO), HALO)
            pltpu.make_async_copy(x_hbm.at[src], xs.at[dst], in_sems.at[k, 0]).start()
            pltpu.make_async_copy(c_hbm.at[src], cs.at[dst], in_sems.at[k, 1]).start()
    if plan.got:
        got_load = pltpu.make_async_copy(got_hbm, got_st, got_sems.at[2])
        got_load.start()
    if grads_on and not first:
        gacc_load = pltpu.make_async_copy(gacc_c, gacc_in, misc_sems.at[8])
        gacc_load.start()

    def wait_piece(k):
        _, dst = piece_place(k)
        pltpu.make_async_copy(x_hbm.at[pl.ds(0, HALO)], xs.at[dst], in_sems.at[k, 0]).wait()
        pltpu.make_async_copy(c_hbm.at[pl.ds(0, HALO)], cs.at[dst], in_sems.at[k, 1]).wait()

    row_iota = lax.broadcasted_iota(jnp.int32, (WINDOW, WINDOW), 0)
    wide_iota = lax.broadcasted_iota(jnp.int32, (WINDOW, 256), 0)

    def mask_cot(start):
        piece = pl.ds(pl.multiple_of(start, WINDOW), WINDOW)
        cs[piece, :] = jnp.where(wide_iota < count_of(start), cs[piece, :].astype(F32), 0.0).astype(BF)

    if grads_on:
        gacc[...] = jnp.zeros_like(gacc)
    for copy in copies:
        copy.wait()
    if first:
        build_weights(side, own_ref, oth_ref, wqkv, wqkv_t, wout_t, wout_p)
    if not first:
        wait_piece(0)
        for b in range(2):
            mask_cot(side * groups * GROUP + b * WINDOW)

    def base_of(i):
        return HALO + i * GROUP + side * (GROUP * groups - 3 * HALO - 2 * GROUP * i)

    def ready_of(base, part):
        return base - HALO + part * HALO + side * (3 * HALO - 2 * HALO * part)

    def result_copies(i):
        start = pl.multiple_of(ready_of(base_of(i), 0) - side * HALO, HALO)
        here = pl.ds(start, GROUP)
        final = pl.ds(pl.multiple_of(origin + start, HALO), GROUP)
        found = [
            pltpu.make_async_copy(keep_o.at[here], out_full.at[final], out_sems.at[i, 0]),
            pltpu.make_async_copy(keep_g.at[here], gn_full.at[final], out_sems.at[i, 1]),
        ]
        if plan.send:
            first_row = (1 - side) * (GROUP if first else 0) + side * HALO
            there = pl.ds(pl.multiple_of(start - first_row, HALO), GROUP)
            found.append(pltpu.make_async_copy(send_st.at[here], send.at[there], out_sems.at[i, 2]))
        return found

    def step(i, with_finish):
        base = pl.multiple_of(base_of(i), HALO)
        here = pl.ds(base, GROUP)
        wait_piece(2 * i + 1)
        wait_piece(2 * i + 2)
        for b in range(4):
            mask_cot(base + b * WINDOW)
        proj = mm(xs[here, :], wqkv[...])
        dctx = mm(cs[here, :], wout_t[...])
        near_in[here, 0:384] = proj[:, 0:384].astype(BF)
        near_in[here, 384:512] = dctx[:, 0:128].astype(BF)
        for j in range(3):
            far_stage[j] = proj[:, 384 + 128 * j : 512 + 128 * j]
        far_stage[3] = dctx[:, 128:256]
        spread = head_masks()

        def far_window(r):
            def load():
                return [far_stage[j, pl.ds(r, WINDOW, stride=4), :].astype(BF) for j in range(4)]

            def mask():
                quarter = row_iota // 32
                limit = jnp.where(
                    quarter < 2,
                    jnp.where(quarter == 0, count_of(base), count_of(base + WINDOW)),
                    jnp.where(quarter == 2, count_of(base + 2 * WINDOW), count_of(base + 3 * WINDOW)),
                )
                return 4 * (row_iota - 32 * quarter) + r < limit

            def store(result):
                for j in range(4):
                    far_res[j, pl.ds(r, WINDOW, stride=4), :] = result[j]

            return Window(load, mask, store, spread)

        def near_window(k):
            start = base - 64 + WINDOW * k + side * (WINDOW + WINDOW * (3 - 2 * k))
            spot = pl.ds(pl.multiple_of(start, 64), WINDOW)

            def load():
                block = near_in[spot, :]
                return [block[:, 128 * j : 128 * j + 128] for j in range(4)]

            def mask():
                limit = jnp.where(row_iota < 64, count_of(start - 64) - 64, count_of(start + 64) + 64)
                return row_iota < limit

            def store(result):
                for j in range(4):
                    near_out[spot, 128 * j : 128 * j + 128] = result[j].astype(BF)

            return Window(load, mask, store, spread)

        def finish(part):
            start = pl.multiple_of(ready_of(base, part), HALO)
            ready = pl.ds(start, HALO)
            near = near_out[ready, :]
            far = far_out[ready, :]
            ctx = jnp.concatenate([near[:, :128], far[:, :128]], 1)
            grads = jnp.concatenate([near[:, 128:], far[:, 128:]], 1)
            wp, wt = (wout_p, wqkv_t) if plan.send else (wout_p.at[:, pl.ds(0, 128)], wqkv_t.at[:, pl.ds(0, 128)])
            out = mm(ctx, wp[...])
            parts = []
            for q in range(2):
                rows = slice(q * WINDOW, (q + 1) * WINDOW)
                keep = wide_iota[:, : out.shape[1]] < count_of(start + q * WINDOW)
                parts.append(jnp.where(keep, out[rows], 0.0))
            out = jnp.concatenate(parts, 0).astype(BF)
            gn = mm(grads, wt[...]).astype(BF)
            keep_o[ready, :] = out[:, :128]
            keep_g[ready, :] = gn[:, :128]
            if plan.send:
                send_st[ready, 0:128] = out[:, 128:]
                send_st[ready, 128:256] = gn[:, 128:]
            if grads_on:
                gacc[:, 0:768] += mm(turned_x[part], grads)
                gacc[:, 768:1024] += mm(turned_c[part], ctx)

        if with_finish and grads_on:
            halves = [pl.ds(pl.multiple_of(ready_of(base, p), HALO), HALO) for p in range(2)]
            turned_x = [xs[half, :].T for half in halves]
            turned_c = [cs[half, :].T for half in halves]

        line = [near_window(0)] + [far_window(r) for r in range(4)] + [near_window(k) for k in range(1, 4)]
        count = len(line)
        for t in range(count + 2):
            if t < count:
                line[t].scores()
            if 1 <= t <= count:
                line[t - 1].softmax()
            if t >= 2:
                line[t - 2].outputs()
            if t == 3 and with_finish:
                finish(0)
            if t == 6:
                for j in range(4):
                    far_out[here, 128 * j : 128 * j + 128] = far_res[j].astype(BF)
        if with_finish:
            finish(1)
            for copy in result_copies(i):
                copy.start()

    start = 0
    if first:
        step(0, False)
        start = 1
    if plan.got:
        got_load.wait()
        row, size = plan.got
        theirs = side * row + (1 - side) * (slab - row - size)
        theirs = pl.ds(pl.multiple_of(theirs, HALO), size)
        got_copies = (
            pltpu.make_async_copy(got_st.at[:, pl.ds(0, 128)], out_full.at[theirs], got_sems.at[0]),
            pltpu.make_async_copy(got_st.at[:, pl.ds(128, 128)], gn_full.at[theirs], got_sems.at[1]),
        )
        for copy in got_copies:
            copy.start()

    def loop_body(i, _):
        step(i, True)
        return 0

    lax.fori_loop(start, groups, loop_body, 0)

    passed = []
    if plan.carry:
        for k, buffer in enumerate((near_in, near_out, far_out)):
            passed.append(pltpu.make_async_copy(buffer.at[carry_out], carry_n[k], misc_sems.at[k]))
            passed[-1].start()
    if grads_on:
        if not first:
            gacc_load.wait()
            gacc[...] = gacc[...] + gacc_in[...]
        if plan.last:
            turned_out = gacc[:, 768:1024].T
            for pos in range(2):
                half = side if pos == 0 else 1 - side
                for j in range(3):
                    near = gacc[:, 128 * j + 64 * pos : 128 * j + 64 * pos + 64]
                    far = gacc[:, 384 + 128 * j + 64 * pos : 384 + 128 * j + 64 * pos + 64]
                    g_out[half, 256 * j : 256 * j + 256, :] = (jnp.concatenate([near, far], 1) * norm).astype(BF)
                rows = [turned_out[128 * part + 64 * pos : 128 * part + 64 * pos + 64] for part in range(2)]
                rows = jnp.concatenate(rows, 0).reshape(16, 8, 256)
                rows = jnp.concatenate([rows[:, :, :128], rows[:, :, 128:]], 1).reshape(256, 128)
                g_out[half, 768:1024, :] = (rows * norm).astype(BF)
        else:
            passed.append(pltpu.make_async_copy(gacc, g_out, misc_sems.at[3]))
            passed[-1].start()
    for copy in passed:
        copy.wait()
    for i in range(1 if first else 0, groups):
        for copy in result_copies(i):
            copy.wait()
    if plan.got:
        for copy in got_copies:
            copy.wait()


def chunk_call(plan, norm, counts, nodes_in, cotangent, halo, weights, carry, gacc, fulls, got):
    vmem = pl.BlockSpec(memory_space=pltpu.VMEM)
    hbm = pl.BlockSpec(memory_space=pltpu.HBM)
    either = pl.BlockSpec(memory_space=pl.ANY)
    slab = nodes_in.shape[0]
    groups, first, grads_on = plan.groups, plan.first, not plan.beyond
    buffer = HALO + groups * GROUP
    sds = jax.ShapeDtypeStruct
    weight_shapes = [(256, 768), (768, 256), (256, 256), (256, 256)]
    aliases = {}
    if first:
        args = [counts, nodes_in, cotangent, halo] + list(weights)
        in_specs = [hbm] * 3 + [either] * 3
    else:
        args = [counts, nodes_in, cotangent] + list(weights) + list(carry) + ([gacc] if grads_on else []) + list(fulls)
        in_specs = [hbm] * 3 + [either] * (len(args) - 5) + [hbm] * 2
        aliases = {len(args) - 2: 0, len(args) - 1: 1}
    if got is not None:
        args.append(got)
        in_specs.append(either)
    out_shape = [sds((slab, 128), BF), sds((slab, 128), BF)]
    if plan.send:
        out_shape.append(sds((plan.rows, 256), BF))
    out_specs = [hbm] * 2 + [either] * (len(out_shape) - 2)
    if first:
        out_shape += [sds(shape, BF) for shape in weight_shapes]
        out_specs += [vmem] * 4
    if plan.carry:
        out_shape += [sds((HALO, 512), BF)] * 3
        out_specs += [either] * 3
    if grads_on:
        out_shape.append(sds((2, 1024, 128), BF) if plan.last else sds((256, 1024), F32))
        out_specs.append(vmem if plan.last else either)
    scratch = [
        pltpu.VMEM((buffer, 256), BF),
        pltpu.VMEM((buffer, 256), BF),
        pltpu.VMEM((buffer, 512), BF),
        pltpu.VMEM((buffer, 512), BF),
        pltpu.VMEM((buffer, 512), BF),
        pltpu.VMEM((4, GROUP, 128), F32),
        pltpu.VMEM((4, GROUP, 128), F32),
        pltpu.VMEM((256, 1024), F32),
        pltpu.VMEM((256, 1024), F32),
        pltpu.VMEM((buffer, 128), BF),
        pltpu.VMEM((buffer, 128), BF),
        pltpu.VMEM((buffer, 256), BF),
        pltpu.SMEM((counts.shape[0],), jnp.int32),
        pltpu.SemaphoreType.DMA((2 * groups + 1, 2)),
        pltpu.SemaphoreType.DMA((9,)),
        pltpu.SemaphoreType.DMA((groups, 3)),
    ]
    if first:
        scratch += [pltpu.VMEM((1024, 128), BF)] * 2
    else:
        scratch += [pltpu.VMEM(shape, BF) for shape in weight_shapes]
    if got is not None:
        scratch += [pltpu.VMEM(got.shape, BF), pltpu.SemaphoreType.DMA((3,))]
    outs = pl.pallas_call(
        functools.partial(chunk_kernel, plan, norm),
        out_shape=out_shape,
        in_specs=in_specs,
        out_specs=out_specs,
        input_output_aliases=aliases,
        scratch_shapes=scratch,
        compiler_params=pltpu.CompilerParams(vmem_limit_bytes=VMEM_LIMIT),
        cost_estimate=pl.CostEstimate(
            flops=plan.rows * plan.cost, bytes_accessed=plan.rows * 1000, transcendentals=0
        ),
    )(*args)
    outs = list(outs)
    fulls, rest = outs[:2], outs[2:]
    sent = rest.pop(0) if plan.send else None
    if first:
        weights, rest = rest[:4], rest[4:]
    carry, rest = (rest[:3], rest[3:]) if plan.carry else (None, rest)
    gacc = rest[0] if grads_on else None
    return fulls, sent, weights, carry, gacc


def pack_kernel(x_hbm, c_hbm, wq, wk, wv, wo, packed, rims, stage, sems):
    side = lax.axis_index("head").astype(jnp.int32)
    rows = pl.ds(pl.multiple_of((1 - side) * (x_hbm.shape[0] - HALO), HALO), HALO)
    loads = [
        pltpu.make_async_copy(x_hbm.at[rows], rims.at[:, pl.ds(0, 256)], sems.at[0]),
        pltpu.make_async_copy(c_hbm.at[rows], rims.at[:, pl.ds(256, 256)], sems.at[1]),
        pltpu.make_async_copy(wq, packed.at[pl.ds(0, 256)], sems.at[2]),
        pltpu.make_async_copy(wk, packed.at[pl.ds(256, 256)], sems.at[3]),
        pltpu.make_async_copy(wv, packed.at[pl.ds(512, 256)], sems.at[4]),
        pltpu.make_async_copy(wo, stage, sems.at[5]),
    ]
    for copy in loads:
        copy.start()
    for copy in loads:
        copy.wait()
    packed[768:896, :] = stage[:, 0:128]
    packed[896:1024, :] = stage[:, 128:256]


def pack_call(nodes_in, cotangent, w_query, w_key, w_value, w_out):
    vmem = pl.BlockSpec(memory_space=pltpu.VMEM)
    hbm = pl.BlockSpec(memory_space=pltpu.HBM)
    return pl.pallas_call(
        pack_kernel,
        out_shape=(jax.ShapeDtypeStruct((1024, 128), BF), jax.ShapeDtypeStruct((HALO, 512), BF)),
        in_specs=[hbm] * 6,
        out_specs=(vmem, vmem),
        scratch_shapes=[pltpu.VMEM(w_out.shape, BF), pltpu.SemaphoreType.DMA((6,))],
    )(nodes_in, cotangent, w_query, w_key, w_value, w_out)


def per_device(nodes_in, cotangent, w_query, w_key, w_value, w_out, counts):
    row_count = nodes_in.shape[0]
    gz, heads, tiles = lax.axis_size("gz"), lax.axis_size("head"), lax.axis_size("tile")
    places = gz * tiles
    swap = [(0, 1), (1, 0)]

    def flat(p, h):
        return (p // tiles * heads + h) * tiles + p % tiles

    own, rims = pack_call(nodes_in, cotangent, w_query, w_key, w_value, w_out)
    oth = lax.ppermute(own, "head", swap)
    route = [(flat(p, 0), flat((p + 1) % places, 0)) for p in range(places)]
    route += [(flat(p, 1), flat((p - 1) % places, 1)) for p in range(places)]
    halo = lax.ppermute(rims, ("gz", "head", "tile"), route)

    norm = float(row_count * places) ** (-0.5)
    weights, carry, gacc, fulls = (own, oth), None, None, None
    waiting, first_group, row = [], 0, 0
    own_count, beyond_count = len(OWN_CALLS), len(BEYOND_CALLS)

    for n, groups in enumerate(OWN_CALLS + BEYOND_CALLS):
        first, beyond = n == 0, n >= own_count
        last, end = n == own_count - 1, n == own_count + beyond_count - 1
        send = n < own_count - 1
        got_rows, got = waiting.pop(0) if waiting and n > 1 else (None, None)
        spot = None if got is None else (got_rows, got.shape[0])
        plan = Plan(first_group, groups, first, last, beyond, send, not end, spot)
        fulls, sent, weights, carry, gacc = chunk_call(
            plan, norm, counts, nodes_in, cotangent, halo, weights, carry, gacc, fulls, got
        )
        if send:
            waiting.append((row, lax.ppermute(sent, "head", swap)))
        if last:
            grads = gacc.reshape(heads * places, 1024 // places, 128)
            grads = lax.all_to_all(grads, ("head", "gz", "tile"), 0, 0, tiled=True)
        if n == own_count:
            grads, *fulls = lax.optimization_barrier((grads, *fulls))
        first_group += groups
        row += plan.rows

    share = jnp.sum(grads.astype(F32), axis=0).astype(BF)
    share = jnp.broadcast_to(share[None], (places,) + share.shape)
    whole = lax.all_to_all(share, ("gz", "tile"), 0, 0, tiled=True).reshape(1024, 128).astype(F32)
    grad_out = whole[768:1024].reshape(16, 2, 8, 128).transpose(0, 2, 1, 3).reshape(128, 256)
    return (fulls[0], fulls[1], whole[0:256], whole[256:512], whole[512:768], grad_out)


def solution(mesh):
    return jax.shard_map(
        per_device,
        mesh=mesh,
        in_specs=(
            P(("gz", "tile"), None),
            P(("gz", "tile"), None),
            P(None, "head"),
            P(None, "head"),
            P(None, "head"),
            P("head", None),
            P(),
        ),
        out_specs=(
            P(("gz", "tile"), "head"),
            P(("gz", "tile"), "head"),
            P(None, "head"),
            P(None, "head"),
            P(None, "head"),
            P("head", None),
        ),
        check_vma=False,
    )
```

```python
import functools
import math

import jax
import jax.numpy as jnp
from jax import lax
from jax.experimental import pallas as pl
from jax.experimental.pallas import tpu as pltpu
from jax.sharding import PartitionSpec as P

WINDOW = 128
HALO = 256
GROUP = 512
HEAD_DIM = 32
OWN_CALLS = (4, 5)
BEYOND_CALLS = (3, 2)
SCALE = HEAD_DIM ** (-0.5)
EXP2_SCALE = SCALE * math.log2(math.e)
VMEM_LIMIT = 58 * 1024 * 1024
BF = jnp.bfloat16
F32 = jnp.float32


def mm(a, b):
    return jnp.dot(a, b, preferred_element_type=F32)


def mm_nt(a, b):
    return lax.dot_general(a, b, (((1,), (1,)), ((), ())), preferred_element_type=F32)


def head_masks():
    lane_head = lax.broadcasted_iota(jnp.int32, (WINDOW, WINDOW), 1) // HEAD_DIM
    return [jnp.where(lane_head == h, 1.0, 0.0).astype(BF) for h in range(4)]


class Window:
    def __init__(self, load, mask, store, spread):
        self.load, self.mask, self.store, self.spread = load, mask, store, spread

    def scores(self):
        q, k, v, d = self.load()
        self.keep = self.mask().astype(F32)
        self.q4 = jnp.concatenate([q * m for m in self.spread], 0)
        self.d4 = jnp.concatenate([d * m for m in self.spread], 0)
        self.s = mm_nt(k, self.q4)
        self.da = mm_nt(v, self.d4)
        self.k_t, self.v_t = k.T, v.T

    def softmax(self):
        low, dsc = [], []
        for h in range(4):
            cols = slice(h * WINDOW, (h + 1) * WINDOW)
            e = jnp.exp2(self.s[:, cols] * EXP2_SCALE) * self.keep
            a = e * (1.0 / jnp.sum(e, axis=0, keepdims=True))
            d = self.da[:, cols]
            center = jnp.sum(a * d, axis=0, keepdims=True)
            low.append(a.astype(BF))
            dsc.append((a * (d - center)).astype(BF))
        self.low = jnp.concatenate(low, 1)
        self.dsc = jnp.concatenate(dsc, 1)

    def outputs(self):
        ctx_t, dq_t = [], []
        for pair in range(2):
            rows = slice(pair * 64, pair * 64 + 64)
            cols = slice(pair * 256, pair * 256 + 256)
            c2 = mm(self.v_t[rows], self.low[:, cols])
            q2 = mm(self.k_t[rows], self.dsc[:, cols])
            ctx_t += [c2[:32, :128], c2[32:, 128:]]
            dq_t += [q2[:32, :128], q2[32:, 128:]]
        dv = mm(self.low, self.d4)
        dk = mm(self.dsc, self.q4) * SCALE
        ctx = jnp.concatenate(ctx_t, 0).T
        dq = jnp.concatenate(dq_t, 0).T * SCALE
        self.store((ctx, dq, dk, dv))


def build_weights(side, own_ref, oth_ref, wqkv, wqkv_t, wout_t, wout_p):
    for part in range(2):
        cols = slice(part * 64, part * 64 + 64)
        for j in range(3):
            in_rows = slice(j * 256, j * 256 + 256)
            wqkv[:, part * 384 + j * 128 : part * 384 + j * 128 + 128] = jnp.concatenate(
                [own_ref[in_rows, cols], oth_ref[in_rows, cols]], 1
            )
        for pos, half in enumerate((own_ref, oth_ref)):
            dst_rows = slice(part * 128 + pos * 64, part * 128 + pos * 64 + 64)
            for col in range(2):
                natural = half[768 + 128 * col + part * 64 : 768 + 128 * col + part * 64 + 64, :]
                wout_t[dst_rows, col * 128 : col * 128 + 128] = natural
                turn = jnp.where(side == 0, col, 1 - col)
                start = pl.multiple_of(768 + 128 * turn + part * 64, 64)
                wout_p[dst_rows, col * 128 : col * 128 + 128] = half[pl.ds(start, 64), :]
    wout_t[...] = wout_t[...].T
    wqkv_t[:, 0:128] = wqkv[pl.ds(pl.multiple_of(side * 128, 128), 128), :].T
    wqkv_t[:, 128:256] = wqkv[pl.ds(pl.multiple_of((1 - side) * 128, 128), 128), :].T


class Plan:
    def __init__(self, first_group, groups, first, last, beyond, send, carry, got):
        self.first_group, self.groups = first_group, groups
        self.first, self.last, self.beyond, self.send = first, last, beyond, send
        self.carry = carry
        self.got = got
        self.blocks = groups - (1 if first else 0)
        self.cost = 200000 if beyond else 4000000
        self.rows = self.blocks * GROUP


def chunk_kernel(plan, norm, *refs):
    refs = list(refs)
    take = lambda n: [refs.pop(0) for _ in range(n)]
    groups, first = plan.groups, plan.first
    grads_on = not plan.beyond
    counts_hbm, x_hbm, c_hbm = take(3)
    if first:
        halo_hbm, own_hbm, oth_hbm = take(3)
    else:
        weights_c = take(4)
        carry_c = take(3)
        gacc_c = take(1)[0] if grads_on else None
        take(2)
    got_hbm = take(1)[0] if plan.got else None
    out_full, gn_full = take(2)
    send = take(1)[0] if plan.send else None
    if first:
        weights = take(4)
    carry_n = take(3) if plan.carry else None
    g_out = take(1)[0] if grads_on else None
    (xs, cs, near_in, near_out, far_out, far_stage, far_res, gacc, gacc_in, keep_o, keep_g, send_st, counts) = take(13)
    in_sems, misc_sems, out_sems = take(3)
    if first:
        own_ref, oth_ref = take(2)
    else:
        weights = take(4)
    if plan.got:
        got_st, got_sems = take(2)
    wqkv, wqkv_t, wout_t, wout_p = weights

    side = lax.axis_index("head").astype(jnp.int32)
    place = lax.axis_index(("gz", "tile")).astype(jnp.int32)
    total_blocks = counts.shape[0]
    slab = x_hbm.shape[0]
    up = GROUP * plan.first_group - GROUP
    down = slab - HALO - GROUP * (plan.first_group + groups - 1)
    origin = up + side * (down - up)
    first_block = place * (slab // WINDOW) + (origin + GROUP) // WINDOW - GROUP // WINDOW + total_blocks
    carry_in = pl.ds(pl.multiple_of(side * groups * GROUP, HALO), HALO)
    carry_out = pl.ds(pl.multiple_of((1 - side) * groups * GROUP, HALO), HALO)

    def count_of(row):
        return counts[lax.rem(first_block + row // WINDOW, total_blocks)]

    def piece_place(k):
        piece = k + side * (2 * groups - 2 * k)
        return piece, pl.ds(pl.multiple_of(piece * HALO, HALO), HALO)

    copies = [pltpu.make_async_copy(counts_hbm, counts, misc_sems.at[0])]
    if first:
        copies.append(pltpu.make_async_copy(own_hbm, own_ref, misc_sems.at[1]))
        copies.append(pltpu.make_async_copy(oth_hbm, oth_ref, misc_sems.at[2]))
    else:
        for k in range(4):
            copies.append(pltpu.make_async_copy(weights_c[k], weights[k], misc_sems.at[1 + k]))
        for k, buffer in enumerate((near_in, near_out, far_out)):
            copies.append(pltpu.make_async_copy(carry_c[k], buffer.at[carry_in], misc_sems.at[5 + k]))
    for copy in copies:
        copy.start()
    for k in range(1 if first else 0, 2 * groups + 1):
        piece, dst = piece_place(k)
        if first and k == 1:
            pltpu.make_async_copy(halo_hbm.at[:, pl.ds(0, 256)], xs.at[dst], in_sems.at[k, 0]).start()
            pltpu.make_async_copy(halo_hbm.at[:, pl.ds(256, 256)], cs.at[dst], in_sems.at[k, 1]).start()
        else:
            src = pl.ds(pl.multiple_of(origin + piece * HALO, HALO), HALO)
            pltpu.make_async_copy(x_hbm.at[src], xs.at[dst], in_sems.at[k, 0]).start()
            pltpu.make_async_copy(c_hbm.at[src], cs.at[dst], in_sems.at[k, 1]).start()
    if plan.got:
        got_load = pltpu.make_async_copy(got_hbm, got_st, got_sems.at[2])
        got_load.start()
    if grads_on and not first:
        gacc_load = pltpu.make_async_copy(gacc_c, gacc_in, misc_sems.at[8])
        gacc_load.start()

    def wait_piece(k):
        _, dst = piece_place(k)
        pltpu.make_async_copy(x_hbm.at[pl.ds(0, HALO)], xs.at[dst], in_sems.at[k, 0]).wait()
        pltpu.make_async_copy(c_hbm.at[pl.ds(0, HALO)], cs.at[dst], in_sems.at[k, 1]).wait()

    row_iota = lax.broadcasted_iota(jnp.int32, (WINDOW, WINDOW), 0)
    wide_iota = lax.broadcasted_iota(jnp.int32, (WINDOW, 256), 0)

    def mask_cot(start):
        piece = pl.ds(pl.multiple_of(start, WINDOW), WINDOW)
        cs[piece, :] = jnp.where(wide_iota < count_of(start), cs[piece, :].astype(F32), 0.0).astype(BF)

    if grads_on:
        gacc[...] = jnp.zeros_like(gacc)
    for copy in copies:
        copy.wait()
    if first:
        build_weights(side, own_ref, oth_ref, wqkv, wqkv_t, wout_t, wout_p)
    if not first:
        wait_piece(0)
        for b in range(2):
            mask_cot(side * groups * GROUP + b * WINDOW)

    def base_of(i):
        return HALO + i * GROUP + side * (GROUP * groups - 3 * HALO - 2 * GROUP * i)

    def ready_of(base, part):
        return base - HALO + part * HALO + side * (3 * HALO - 2 * HALO * part)

    def half_copies(i, part):
        start = pl.multiple_of(ready_of(base_of(i), part), HALO)
        here = pl.ds(start, HALO)
        final = pl.ds(pl.multiple_of(origin + start, HALO), HALO)
        found = [
            pltpu.make_async_copy(keep_o.at[here], out_full.at[final], out_sems.at[i, 3 * part]),
            pltpu.make_async_copy(keep_g.at[here], gn_full.at[final], out_sems.at[i, 3 * part + 1]),
        ]
        if plan.send:
            first_row = (1 - side) * (GROUP if first else 0) + side * HALO
            there = pl.ds(pl.multiple_of(start - first_row, HALO), HALO)
            found.append(pltpu.make_async_copy(send_st.at[here], send.at[there], out_sems.at[i, 3 * part + 2]))
        return found

    def wait_group(i):
        wait_piece(2 * i + 1)
        wait_piece(2 * i + 2)

    def project(i, slot):
        base = pl.multiple_of(base_of(i), HALO)
        here = pl.ds(base, GROUP)
        for b in range(4):
            mask_cot(base + b * WINDOW)
        proj = mm(xs[here, :], wqkv[...])
        dctx = mm(cs[here, :], wout_t[...])
        near_in[here, 0:384] = proj[:, 0:384].astype(BF)
        near_in[here, 384:512] = dctx[:, 0:128].astype(BF)
        for j in range(3):
            far_stage[slot, j] = proj[:, 384 + 128 * j : 512 + 128 * j]
        far_stage[slot, 3] = dctx[:, 128:256]

    def turn(i, part):
        half = pl.ds(pl.multiple_of(ready_of(base_of(i), part), HALO), HALO)
        return (xs[half, :].T, cs[half, :].T) if grads_on else None

    def finish(i, part, turned):
        start = pl.multiple_of(ready_of(base_of(i), part), HALO)
        ready = pl.ds(start, HALO)
        near = near_out[ready, :]
        far = far_out[ready, :]
        ctx = jnp.concatenate([near[:, :128], far[:, :128]], 1)
        grads = jnp.concatenate([near[:, 128:], far[:, 128:]], 1)
        wp, wt = (wout_p, wqkv_t) if plan.send else (wout_p.at[:, pl.ds(0, 128)], wqkv_t.at[:, pl.ds(0, 128)])
        out = mm(ctx, wp[...])
        parts = []
        for q in range(2):
            rows = slice(q * WINDOW, (q + 1) * WINDOW)
            keep = wide_iota[:, : out.shape[1]] < count_of(start + q * WINDOW)
            parts.append(jnp.where(keep, out[rows], 0.0))
        out = jnp.concatenate(parts, 0).astype(BF)
        gn = mm(grads, wt[...]).astype(BF)
        keep_o[ready, :] = out[:, :128]
        keep_g[ready, :] = gn[:, :128]
        if plan.send:
            send_st[ready, 0:128] = out[:, 128:]
            send_st[ready, 128:256] = gn[:, 128:]
        if grads_on:
            gacc[:, 0:768] += mm(turned[0], grads)
            gacc[:, 768:1024] += mm(turned[1], ctx)

    def step(i, before, with_finish):
        base = pl.multiple_of(base_of(i), HALO)
        here = pl.ds(base, GROUP)
        following = jnp.minimum(i + 1, groups - 1)
        slot = lax.rem(i, 2)
        if isinstance(i, int):
            if i + 1 < groups:
                wait_group(i + 1)
        else:

            @pl.when(i + 1 < groups)
            def _():
                wait_group(i + 1)

        spread = head_masks()

        def far_window(r):
            def load():
                return [far_stage[slot, j, pl.ds(r, WINDOW, stride=4), :].astype(BF) for j in range(4)]

            def mask():
                quarter = row_iota // 32
                limit = jnp.where(
                    quarter < 2,
                    jnp.where(quarter == 0, count_of(base), count_of(base + WINDOW)),
                    jnp.where(quarter == 2, count_of(base + 2 * WINDOW), count_of(base + 3 * WINDOW)),
                )
                return 4 * (row_iota - 32 * quarter) + r < limit

            def store(result):
                for j in range(4):
                    far_res[j, pl.ds(r, WINDOW, stride=4), :] = result[j]

            return Window(load, mask, store, spread)

        def near_window(k):
            start = base - 64 + WINDOW * k + side * (WINDOW + WINDOW * (3 - 2 * k))
            spot = pl.ds(pl.multiple_of(start, 64), WINDOW)

            def load():
                block = near_in[spot, :]
                return [block[:, 128 * j : 128 * j + 128] for j in range(4)]

            def mask():
                limit = jnp.where(row_iota < 64, count_of(start - 64) - 64, count_of(start + 64) + 64)
                return row_iota < limit

            def store(result):
                for j in range(4):
                    near_out[spot, 128 * j : 128 * j + 128] = result[j].astype(BF)

            return Window(load, mask, store, spread)

        if before:
            turned_before = turn(i - 1, 1)
        if with_finish:
            turned = turn(i, 0)

        line = [near_window(0)] + [far_window(r) for r in range(4)] + [near_window(k) for k in range(1, 4)]
        count = len(line)
        for t in range(count + 2):
            if t < count:
                line[t].scores()
            if 1 <= t <= count:
                line[t - 1].softmax()
            if t >= 2:
                line[t - 2].outputs()
            if t == 1 and before:
                finish(i - 1, 1, turned_before)
            if t == 3 and with_finish:
                finish(i, 0, turned)
            if t == 6:
                for j in range(4):
                    far_out[here, 128 * j : 128 * j + 128] = far_res[j].astype(BF)
            if t == 8:
                project(following, 1 - slot)
        halves = ([(i - 1, 1)] if before else []) + ([(i, 0)] if with_finish else [])
        for group, part in halves:
            for copy in half_copies(group, part):
                copy.start()

    wait_group(0)
    project(0, 0)
    start = 1
    step(0, False, not first)
    if first:
        step(1, False, True)
        start = 2
    if plan.got:
        got_load.wait()
        row, size = plan.got
        theirs = side * row + (1 - side) * (slab - row - size)
        theirs = pl.ds(pl.multiple_of(theirs, HALO), size)
        got_copies = (
            pltpu.make_async_copy(got_st.at[:, pl.ds(0, 128)], out_full.at[theirs], got_sems.at[0]),
            pltpu.make_async_copy(got_st.at[:, pl.ds(128, 128)], gn_full.at[theirs], got_sems.at[1]),
        )
        for copy in got_copies:
            copy.start()

    def loop_body(i, _):
        step(i, True, True)
        return 0

    lax.fori_loop(start, groups, loop_body, 0)
    finish(groups - 1, 1, turn(groups - 1, 1))
    for copy in half_copies(groups - 1, 1):
        copy.start()

    passed = []
    if plan.carry:
        for k, buffer in enumerate((near_in, near_out, far_out)):
            passed.append(pltpu.make_async_copy(buffer.at[carry_out], carry_n[k], misc_sems.at[k]))
            passed[-1].start()
    if grads_on:
        if not first:
            gacc_load.wait()
            gacc[...] = gacc[...] + gacc_in[...]
        if plan.last:
            turned_out = gacc[:, 768:1024].T
            for pos in range(2):
                half = side if pos == 0 else 1 - side
                for j in range(3):
                    near = gacc[:, 128 * j + 64 * pos : 128 * j + 64 * pos + 64]
                    far = gacc[:, 384 + 128 * j + 64 * pos : 384 + 128 * j + 64 * pos + 64]
                    g_out[half, 256 * j : 256 * j + 256, :] = (jnp.concatenate([near, far], 1) * norm).astype(BF)
                rows = [turned_out[128 * part + 64 * pos : 128 * part + 64 * pos + 64] for part in range(2)]
                rows = jnp.concatenate(rows, 0).reshape(16, 8, 256)
                rows = jnp.concatenate([rows[:, :, :128], rows[:, :, 128:]], 1).reshape(256, 128)
                g_out[half, 768:1024, :] = (rows * norm).astype(BF)
        else:
            passed.append(pltpu.make_async_copy(gacc, g_out, misc_sems.at[3]))
            passed[-1].start()
    for copy in passed:
        copy.wait()
    for i in range(1 if first else 0, groups):
        for part in range(2):
            for copy in half_copies(i, part):
                copy.wait()
    if plan.got:
        for copy in got_copies:
            copy.wait()


def chunk_call(plan, norm, counts, nodes_in, cotangent, halo, weights, carry, gacc, fulls, got):
    vmem = pl.BlockSpec(memory_space=pltpu.VMEM)
    hbm = pl.BlockSpec(memory_space=pltpu.HBM)
    either = pl.BlockSpec(memory_space=pl.ANY)
    slab = nodes_in.shape[0]
    groups, first, grads_on = plan.groups, plan.first, not plan.beyond
    buffer = HALO + groups * GROUP
    sds = jax.ShapeDtypeStruct
    weight_shapes = [(256, 768), (768, 256), (256, 256), (256, 256)]
    aliases = {}
    if first:
        args = [counts, nodes_in, cotangent, halo] + list(weights)
        in_specs = [hbm] * 3 + [either] * 3
    else:
        args = [counts, nodes_in, cotangent] + list(weights) + list(carry) + ([gacc] if grads_on else []) + list(fulls)
        in_specs = [hbm] * 3 + [either] * (len(args) - 5) + [hbm] * 2
        aliases = {len(args) - 2: 0, len(args) - 1: 1}
    if got is not None:
        args.append(got)
        in_specs.append(either)
    out_shape = [sds((slab, 128), BF), sds((slab, 128), BF)]
    if plan.send:
        out_shape.append(sds((plan.rows, 256), BF))
    out_specs = [hbm] * 2 + [either] * (len(out_shape) - 2)
    if first:
        out_shape += [sds(shape, BF) for shape in weight_shapes]
        out_specs += [vmem] * 4
    if plan.carry:
        out_shape += [sds((HALO, 512), BF)] * 3
        out_specs += [either] * 3
    if grads_on:
        out_shape.append(sds((2, 1024, 128), BF) if plan.last else sds((256, 1024), F32))
        out_specs.append(vmem if plan.last else either)
    scratch = [
        pltpu.VMEM((buffer, 256), BF),
        pltpu.VMEM((buffer, 256), BF),
        pltpu.VMEM((buffer, 512), BF),
        pltpu.VMEM((buffer, 512), BF),
        pltpu.VMEM((buffer, 512), BF),
        pltpu.VMEM((2, 4, GROUP, 128), F32),
        pltpu.VMEM((4, GROUP, 128), F32),
        pltpu.VMEM((256, 1024), F32),
        pltpu.VMEM((256, 1024), F32),
        pltpu.VMEM((buffer, 128), BF),
        pltpu.VMEM((buffer, 128), BF),
        pltpu.VMEM((buffer, 256), BF),
        pltpu.SMEM((counts.shape[0],), jnp.int32),
        pltpu.SemaphoreType.DMA((2 * groups + 1, 2)),
        pltpu.SemaphoreType.DMA((9,)),
        pltpu.SemaphoreType.DMA((groups, 6)),
    ]
    if first:
        scratch += [pltpu.VMEM((1024, 128), BF)] * 2
    else:
        scratch += [pltpu.VMEM(shape, BF) for shape in weight_shapes]
    if got is not None:
        scratch += [pltpu.VMEM(got.shape, BF), pltpu.SemaphoreType.DMA((3,))]
    outs = pl.pallas_call(
        functools.partial(chunk_kernel, plan, norm),
        out_shape=out_shape,
        in_specs=in_specs,
        out_specs=out_specs,
        input_output_aliases=aliases,
        scratch_shapes=scratch,
        compiler_params=pltpu.CompilerParams(vmem_limit_bytes=VMEM_LIMIT),
        cost_estimate=pl.CostEstimate(
            flops=plan.rows * plan.cost, bytes_accessed=plan.rows * 1000, transcendentals=0
        ),
    )(*args)
    outs = list(outs)
    fulls, rest = outs[:2], outs[2:]
    sent = rest.pop(0) if plan.send else None
    if first:
        weights, rest = rest[:4], rest[4:]
    carry, rest = (rest[:3], rest[3:]) if plan.carry else (None, rest)
    gacc = rest[0] if grads_on else None
    return fulls, sent, weights, carry, gacc


def pack_kernel(x_hbm, c_hbm, wq, wk, wv, wo, packed, rims, stage, sems):
    side = lax.axis_index("head").astype(jnp.int32)
    rows = pl.ds(pl.multiple_of((1 - side) * (x_hbm.shape[0] - HALO), HALO), HALO)
    loads = [
        pltpu.make_async_copy(x_hbm.at[rows], rims.at[:, pl.ds(0, 256)], sems.at[0]),
        pltpu.make_async_copy(c_hbm.at[rows], rims.at[:, pl.ds(256, 256)], sems.at[1]),
        pltpu.make_async_copy(wq, packed.at[pl.ds(0, 256)], sems.at[2]),
        pltpu.make_async_copy(wk, packed.at[pl.ds(256, 256)], sems.at[3]),
        pltpu.make_async_copy(wv, packed.at[pl.ds(512, 256)], sems.at[4]),
        pltpu.make_async_copy(wo, stage, sems.at[5]),
    ]
    for copy in loads:
        copy.start()
    for copy in loads:
        copy.wait()
    packed[768:896, :] = stage[:, 0:128]
    packed[896:1024, :] = stage[:, 128:256]


def pack_call(nodes_in, cotangent, w_query, w_key, w_value, w_out):
    vmem = pl.BlockSpec(memory_space=pltpu.VMEM)
    hbm = pl.BlockSpec(memory_space=pltpu.HBM)
    return pl.pallas_call(
        pack_kernel,
        out_shape=(jax.ShapeDtypeStruct((1024, 128), BF), jax.ShapeDtypeStruct((HALO, 512), BF)),
        in_specs=[hbm] * 6,
        out_specs=(vmem, vmem),
        scratch_shapes=[pltpu.VMEM(w_out.shape, BF), pltpu.SemaphoreType.DMA((6,))],
    )(nodes_in, cotangent, w_query, w_key, w_value, w_out)


def per_device(nodes_in, cotangent, w_query, w_key, w_value, w_out, counts):
    row_count = nodes_in.shape[0]
    gz, heads, tiles = lax.axis_size("gz"), lax.axis_size("head"), lax.axis_size("tile")
    places = gz * tiles
    swap = [(0, 1), (1, 0)]

    def flat(p, h):
        return (p // tiles * heads + h) * tiles + p % tiles

    own, rims = pack_call(nodes_in, cotangent, w_query, w_key, w_value, w_out)
    oth = lax.ppermute(own, "head", swap)
    route = [(flat(p, 0), flat((p + 1) % places, 0)) for p in range(places)]
    route += [(flat(p, 1), flat((p - 1) % places, 1)) for p in range(places)]
    halo = lax.ppermute(rims, ("gz", "head", "tile"), route)

    norm = float(row_count * places) ** (-0.5)
    weights, carry, gacc, fulls = (own, oth), None, None, None
    waiting, first_group, row = [], 0, 0
    own_count, beyond_count = len(OWN_CALLS), len(BEYOND_CALLS)

    for n, groups in enumerate(OWN_CALLS + BEYOND_CALLS):
        first, beyond = n == 0, n >= own_count
        last, end = n == own_count - 1, n == own_count + beyond_count - 1
        send = n < own_count - 1
        got_rows, got = waiting.pop(0) if waiting and n > 1 else (None, None)
        spot = None if got is None else (got_rows, got.shape[0])
        plan = Plan(first_group, groups, first, last, beyond, send, not end, spot)
        fulls, sent, weights, carry, gacc = chunk_call(
            plan, norm, counts, nodes_in, cotangent, halo, weights, carry, gacc, fulls, got
        )
        if send:
            waiting.append((row, lax.ppermute(sent, "head", swap)))
        if last:
            grads = gacc.reshape(heads * places, 1024 // places, 128)
            grads = lax.all_to_all(grads, ("head", "gz", "tile"), 0, 0, tiled=True)
        if n == own_count:
            grads, *fulls = lax.optimization_barrier((grads, *fulls))
        first_group += groups
        row += plan.rows

    share = jnp.sum(grads.astype(F32), axis=0).astype(BF)
    share = jnp.broadcast_to(share[None], (places,) + share.shape)
    whole = lax.all_to_all(share, ("gz", "tile"), 0, 0, tiled=True).reshape(1024, 128).astype(F32)
    grad_out = whole[768:1024].reshape(16, 2, 8, 128).transpose(0, 2, 1, 3).reshape(128, 256)
    return (fulls[0], fulls[1], whole[0:256], whole[256:512], whole[512:768], grad_out)


def solution(mesh):
    return jax.shard_map(
        per_device,
        mesh=mesh,
        in_specs=(
            P(("gz", "tile"), None),
            P(("gz", "tile"), None),
            P(None, "head"),
            P(None, "head"),
            P(None, "head"),
            P("head", None),
            P(),
        ),
        out_specs=(
            P(("gz", "tile"), "head"),
            P(("gz", "tile"), "head"),
            P(None, "head"),
            P(None, "head"),
            P(None, "head"),
            P("head", None),
        ),
        check_vma=False,
    )
```

```python
import functools
import math

import jax
import jax.numpy as jnp
from jax import lax
from jax.experimental import pallas as pl
from jax.experimental.pallas import tpu as pltpu
from jax.sharding import PartitionSpec as P

WINDOW = 128
HALO = 256
GROUP = 512
HEAD_DIM = 32
OWN_CALLS = (4, 5)
BEYOND_CALLS = (3, 2)
SCALE = HEAD_DIM ** (-0.5)
EXP2_SCALE = SCALE * math.log2(math.e)
VMEM_LIMIT = 58 * 1024 * 1024
BF = jnp.bfloat16
F32 = jnp.float32


def mm(a, b):
    return jnp.dot(a, b, preferred_element_type=F32)


def mm_nt(a, b):
    return lax.dot_general(a, b, (((1,), (1,)), ((), ())), preferred_element_type=F32)


def head_masks():
    lane_head = lax.broadcasted_iota(jnp.int32, (WINDOW, WINDOW), 1) // HEAD_DIM
    return [jnp.where(lane_head == h, 1.0, 0.0).astype(BF) for h in range(4)]


class Window:
    def __init__(self, load, mask, store, spread):
        self.load, self.mask, self.store, self.spread = load, mask, store, spread

    def scores(self):
        q, k, v, d = self.load()
        self.keep = self.mask().astype(F32)
        self.q4 = jnp.concatenate([q * m for m in self.spread], 0)
        self.d4 = jnp.concatenate([d * m for m in self.spread], 0)
        self.s = mm_nt(k, self.q4)
        self.da = mm_nt(v, self.d4)
        self.k_t, self.v_t = k.T, v.T

    def softmax(self):
        low, dsc = [], []
        for h in range(4):
            cols = slice(h * WINDOW, (h + 1) * WINDOW)
            e = jnp.exp2(self.s[:, cols] * EXP2_SCALE) * self.keep
            a = e * (1.0 / jnp.sum(e, axis=0, keepdims=True))
            d = self.da[:, cols]
            center = jnp.sum(a * d, axis=0, keepdims=True)
            low.append(a.astype(BF))
            dsc.append((a * (d - center)).astype(BF))
        self.low = jnp.concatenate(low, 1)
        self.dsc = jnp.concatenate(dsc, 1)

    def outputs(self):
        ctx_t, dq_t = [], []
        for pair in range(2):
            rows = slice(pair * 64, pair * 64 + 64)
            cols = slice(pair * 256, pair * 256 + 256)
            c2 = mm(self.v_t[rows], self.low[:, cols])
            q2 = mm(self.k_t[rows], self.dsc[:, cols])
            ctx_t += [c2[:32, :128], c2[32:, 128:]]
            dq_t += [q2[:32, :128], q2[32:, 128:]]
        dv = mm(self.low, self.d4)
        dk = mm(self.dsc, self.q4) * SCALE
        ctx = jnp.concatenate(ctx_t, 0).T
        dq = jnp.concatenate(dq_t, 0).T * SCALE
        self.store((ctx, dq, dk, dv))


def build_weights(side, own_ref, oth_ref, wqkv, wqkv_t, wout_t, wout_p):
    for part in range(2):
        cols = slice(part * 64, part * 64 + 64)
        for j in range(3):
            in_rows = slice(j * 256, j * 256 + 256)
            wqkv[:, part * 384 + j * 128 : part * 384 + j * 128 + 128] = jnp.concatenate(
                [own_ref[in_rows, cols], oth_ref[in_rows, cols]], 1
            )
        for pos, half in enumerate((own_ref, oth_ref)):
            dst_rows = slice(part * 128 + pos * 64, part * 128 + pos * 64 + 64)
            for col in range(2):
                natural = half[768 + 128 * col + part * 64 : 768 + 128 * col + part * 64 + 64, :]
                wout_t[dst_rows, col * 128 : col * 128 + 128] = natural
                turn = jnp.where(side == 0, col, 1 - col)
                start = pl.multiple_of(768 + 128 * turn + part * 64, 64)
                wout_p[dst_rows, col * 128 : col * 128 + 128] = half[pl.ds(start, 64), :]
    wout_t[...] = wout_t[...].T
    wqkv_t[:, 0:128] = wqkv[pl.ds(pl.multiple_of(side * 128, 128), 128), :].T
    wqkv_t[:, 128:256] = wqkv[pl.ds(pl.multiple_of((1 - side) * 128, 128), 128), :].T


class Plan:
    def __init__(self, first_group, groups, first, last, beyond, send, carry, got):
        self.first_group, self.groups = first_group, groups
        self.first, self.last, self.beyond, self.send = first, last, beyond, send
        self.carry = carry
        self.got = got
        self.blocks = groups - (1 if first else 0)
        self.cost = 200000 if beyond else 4000000
        self.rows = self.blocks * GROUP


def chunk_kernel(plan, norm, *refs):
    refs = list(refs)
    take = lambda n: [refs.pop(0) for _ in range(n)]
    groups, first = plan.groups, plan.first
    grads_on = not plan.beyond
    counts_hbm, x_hbm, c_hbm = take(3)
    if first:
        halo_hbm, own_hbm, oth_hbm = take(3)
    else:
        weights_c = take(4)
        carry_c = take(3)
        gacc_c = take(1)[0] if grads_on else None
        take(2)
    got_hbm = take(1)[0] if plan.got else None
    out_full, gn_full = take(2)
    send = take(1)[0] if plan.send else None
    if first:
        weights = take(4)
    carry_n = take(3) if plan.carry else None
    g_out = take(1)[0] if grads_on else None
    (xs, cs, near_in, near_out, far_out, far_stage, far_res, gacc, gacc_in, keep_o, keep_g, send_st, counts) = take(13)
    in_sems, misc_sems, out_sems = take(3)
    if first:
        own_ref, oth_ref = take(2)
    else:
        weights = take(4)
    if plan.got:
        got_st, got_sems = take(2)
    wqkv, wqkv_t, wout_t, wout_p = weights

    side = lax.axis_index("head").astype(jnp.int32)
    place = lax.axis_index(("gz", "tile")).astype(jnp.int32)
    total_blocks = counts.shape[0]
    slab = x_hbm.shape[0]
    up = GROUP * plan.first_group - GROUP
    down = slab - HALO - GROUP * (plan.first_group + groups - 1)
    origin = up + side * (down - up)
    first_block = place * (slab // WINDOW) + (origin + GROUP) // WINDOW - GROUP // WINDOW + total_blocks
    carry_in = pl.ds(pl.multiple_of(side * groups * GROUP, HALO), HALO)
    carry_out = pl.ds(pl.multiple_of((1 - side) * groups * GROUP, HALO), HALO)

    def count_of(row):
        return counts[lax.rem(first_block + row // WINDOW, total_blocks)]

    def piece_place(k):
        piece = k + side * (2 * groups - 2 * k)
        return piece, pl.ds(pl.multiple_of(piece * HALO, HALO), HALO)

    copies, late = [pltpu.make_async_copy(counts_hbm, counts, misc_sems.at[0])], []
    if first:
        copies.append(pltpu.make_async_copy(own_hbm, own_ref, misc_sems.at[1]))
        copies.append(pltpu.make_async_copy(oth_hbm, oth_ref, misc_sems.at[2]))
    else:
        for k in range(4):
            use = copies if k in (0, 2) else late
            use.append(pltpu.make_async_copy(weights_c[k], weights[k], misc_sems.at[1 + k]))
        for k, buffer in enumerate((near_in, near_out, far_out)):
            late.append(pltpu.make_async_copy(carry_c[k], buffer.at[carry_in], misc_sems.at[5 + k]))
    for copy in copies:
        copy.start()
    for k in list(range(1, 2 * groups + 1)) + ([] if first else [0]):
        piece, dst = piece_place(k)
        if first and k == 1:
            pltpu.make_async_copy(halo_hbm.at[:, pl.ds(0, 256)], xs.at[dst], in_sems.at[k, 0]).start()
            pltpu.make_async_copy(halo_hbm.at[:, pl.ds(256, 256)], cs.at[dst], in_sems.at[k, 1]).start()
        else:
            src = pl.ds(pl.multiple_of(origin + piece * HALO, HALO), HALO)
            pltpu.make_async_copy(x_hbm.at[src], xs.at[dst], in_sems.at[k, 0]).start()
            pltpu.make_async_copy(c_hbm.at[src], cs.at[dst], in_sems.at[k, 1]).start()
    for copy in late:
        copy.start()
    if plan.got:
        got_load = pltpu.make_async_copy(got_hbm, got_st, got_sems.at[2])
        got_load.start()
    if grads_on and not first:
        gacc_load = pltpu.make_async_copy(gacc_c, gacc_in, misc_sems.at[8])
        gacc_load.start()

    def wait_piece(k):
        _, dst = piece_place(k)
        pltpu.make_async_copy(x_hbm.at[pl.ds(0, HALO)], xs.at[dst], in_sems.at[k, 0]).wait()
        pltpu.make_async_copy(c_hbm.at[pl.ds(0, HALO)], cs.at[dst], in_sems.at[k, 1]).wait()

    row_iota = lax.broadcasted_iota(jnp.int32, (WINDOW, WINDOW), 0)
    wide_iota = lax.broadcasted_iota(jnp.int32, (WINDOW, 256), 0)

    def mask_cot(start):
        piece = pl.ds(pl.multiple_of(start, WINDOW), WINDOW)
        cs[piece, :] = jnp.where(wide_iota < count_of(start), cs[piece, :].astype(F32), 0.0).astype(BF)

    if grads_on:
        gacc[...] = jnp.zeros_like(gacc)
    for copy in copies:
        copy.wait()
    if first:
        build_weights(side, own_ref, oth_ref, wqkv, wqkv_t, wout_t, wout_p)
    def base_of(i):
        return HALO + i * GROUP + side * (GROUP * groups - 3 * HALO - 2 * GROUP * i)

    def ready_of(base, part):
        return base - HALO + part * HALO + side * (3 * HALO - 2 * HALO * part)

    def half_copies(i, part):
        start = pl.multiple_of(ready_of(base_of(i), part), HALO)
        here = pl.ds(start, HALO)
        final = pl.ds(pl.multiple_of(origin + start, HALO), HALO)
        found = [
            pltpu.make_async_copy(keep_o.at[here], out_full.at[final], out_sems.at[i, 3 * part]),
            pltpu.make_async_copy(keep_g.at[here], gn_full.at[final], out_sems.at[i, 3 * part + 1]),
        ]
        if plan.send:
            first_row = (1 - side) * (GROUP if first else 0) + side * HALO
            there = pl.ds(pl.multiple_of(start - first_row, HALO), HALO)
            found.append(pltpu.make_async_copy(send_st.at[here], send.at[there], out_sems.at[i, 3 * part + 2]))
        return found

    def wait_group(i):
        wait_piece(2 * i + 1)
        wait_piece(2 * i + 2)

    def project(i, slot):
        base = pl.multiple_of(base_of(i), HALO)
        here = pl.ds(base, GROUP)
        for b in range(4):
            mask_cot(base + b * WINDOW)
        proj = mm(xs[here, :], wqkv[...])
        dctx = mm(cs[here, :], wout_t[...])
        near_in[here, 0:384] = proj[:, 0:384].astype(BF)
        near_in[here, 384:512] = dctx[:, 0:128].astype(BF)
        for j in range(3):
            far_stage[slot, j] = proj[:, 384 + 128 * j : 512 + 128 * j]
        far_stage[slot, 3] = dctx[:, 128:256]

    def turn(i, part):
        half = pl.ds(pl.multiple_of(ready_of(base_of(i), part), HALO), HALO)
        return (xs[half, :].T, cs[half, :].T) if grads_on else None

    def finish(i, part, turned):
        start = pl.multiple_of(ready_of(base_of(i), part), HALO)
        ready = pl.ds(start, HALO)
        near = near_out[ready, :]
        far = far_out[ready, :]
        ctx = jnp.concatenate([near[:, :128], far[:, :128]], 1)
        grads = jnp.concatenate([near[:, 128:], far[:, 128:]], 1)
        wp, wt = (wout_p, wqkv_t) if plan.send else (wout_p.at[:, pl.ds(0, 128)], wqkv_t.at[:, pl.ds(0, 128)])
        out = mm(ctx, wp[...])
        parts = []
        for q in range(2):
            rows = slice(q * WINDOW, (q + 1) * WINDOW)
            keep = wide_iota[:, : out.shape[1]] < count_of(start + q * WINDOW)
            parts.append(jnp.where(keep, out[rows], 0.0))
        out = jnp.concatenate(parts, 0).astype(BF)
        gn = mm(grads, wt[...]).astype(BF)
        keep_o[ready, :] = out[:, :128]
        keep_g[ready, :] = gn[:, :128]
        if plan.send:
            send_st[ready, 0:128] = out[:, 128:]
            send_st[ready, 128:256] = gn[:, 128:]
        if grads_on:
            gacc[:, 0:768] += mm(turned[0], grads)
            gacc[:, 768:1024] += mm(turned[1], ctx)

    def step(i, before, with_finish):
        base = pl.multiple_of(base_of(i), HALO)
        here = pl.ds(base, GROUP)
        following = jnp.minimum(i + 1, groups - 1)
        slot = lax.rem(i, 2)
        if isinstance(i, int):
            if i + 1 < groups:
                wait_group(i + 1)
        else:

            @pl.when(i + 1 < groups)
            def _():
                wait_group(i + 1)

        spread = head_masks()

        def far_window(r):
            def load():
                return [far_stage[slot, j, pl.ds(r, WINDOW, stride=4), :].astype(BF) for j in range(4)]

            def mask():
                quarter = row_iota // 32
                limit = jnp.where(
                    quarter < 2,
                    jnp.where(quarter == 0, count_of(base), count_of(base + WINDOW)),
                    jnp.where(quarter == 2, count_of(base + 2 * WINDOW), count_of(base + 3 * WINDOW)),
                )
                return 4 * (row_iota - 32 * quarter) + r < limit

            def store(result):
                for j in range(4):
                    far_res[j, pl.ds(r, WINDOW, stride=4), :] = result[j]

            return Window(load, mask, store, spread)

        def near_window(k):
            start = base - 64 + WINDOW * k + side * (WINDOW + WINDOW * (3 - 2 * k))
            spot = pl.ds(pl.multiple_of(start, 64), WINDOW)

            def load():
                block = near_in[spot, :]
                return [block[:, 128 * j : 128 * j + 128] for j in range(4)]

            def mask():
                limit = jnp.where(row_iota < 64, count_of(start - 64) - 64, count_of(start + 64) + 64)
                return row_iota < limit

            def store(result):
                for j in range(4):
                    near_out[spot, 128 * j : 128 * j + 128] = result[j].astype(BF)

            return Window(load, mask, store, spread)

        if before:
            turned_before = turn(i - 1, 1)
        if with_finish:
            turned = turn(i, 0)

        line = [near_window(0)] + [far_window(r) for r in range(4)] + [near_window(k) for k in range(1, 4)]
        count = len(line)
        for t in range(count + 2):
            if t < count:
                line[t].scores()
            if 1 <= t <= count:
                line[t - 1].softmax()
            if t >= 2:
                line[t - 2].outputs()
            if t == 1 and before:
                finish(i - 1, 1, turned_before)
            if t == 3 and with_finish:
                finish(i, 0, turned)
            if t == 6:
                for j in range(4):
                    far_out[here, 128 * j : 128 * j + 128] = far_res[j].astype(BF)
            if t == 8:
                project(following, 1 - slot)
        halves = ([(i - 1, 1)] if before else []) + ([(i, 0)] if with_finish else [])
        for group, part in halves:
            for copy in half_copies(group, part):
                copy.start()

    wait_group(0)
    project(0, 0)
    for copy in late:
        copy.wait()
    if not first:
        wait_piece(0)
        for b in range(2):
            mask_cot(side * groups * GROUP + b * WINDOW)
    start = 1
    step(0, False, not first)
    if first:
        step(1, False, True)
        start = 2
    if plan.got:
        got_load.wait()
        row, size = plan.got
        theirs = side * row + (1 - side) * (slab - row - size)
        theirs = pl.ds(pl.multiple_of(theirs, HALO), size)
        got_copies = (
            pltpu.make_async_copy(got_st.at[:, pl.ds(0, 128)], out_full.at[theirs], got_sems.at[0]),
            pltpu.make_async_copy(got_st.at[:, pl.ds(128, 128)], gn_full.at[theirs], got_sems.at[1]),
        )
        for copy in got_copies:
            copy.start()

    def loop_body(i, _):
        step(i, True, True)
        return 0

    lax.fori_loop(start, groups, loop_body, 0)
    finish(groups - 1, 1, turn(groups - 1, 1))
    for copy in half_copies(groups - 1, 1):
        copy.start()

    passed = []
    if plan.carry:
        for k, buffer in enumerate((near_in, near_out, far_out)):
            passed.append(pltpu.make_async_copy(buffer.at[carry_out], carry_n[k], misc_sems.at[k]))
            passed[-1].start()
    if grads_on:
        if not first:
            gacc_load.wait()
            gacc[...] = gacc[...] + gacc_in[...]
        if plan.last:
            turned_out = gacc[:, 768:1024].T
            for pos in range(2):
                half = side if pos == 0 else 1 - side
                for j in range(3):
                    near = gacc[:, 128 * j + 64 * pos : 128 * j + 64 * pos + 64]
                    far = gacc[:, 384 + 128 * j + 64 * pos : 384 + 128 * j + 64 * pos + 64]
                    g_out[half, 256 * j : 256 * j + 256, :] = (jnp.concatenate([near, far], 1) * norm).astype(BF)
                rows = [turned_out[128 * part + 64 * pos : 128 * part + 64 * pos + 64] for part in range(2)]
                rows = jnp.concatenate(rows, 0).reshape(16, 8, 256)
                rows = jnp.concatenate([rows[:, :, :128], rows[:, :, 128:]], 1).reshape(256, 128)
                g_out[half, 768:1024, :] = (rows * norm).astype(BF)
        else:
            passed.append(pltpu.make_async_copy(gacc, g_out, misc_sems.at[3]))
            passed[-1].start()
    for copy in passed:
        copy.wait()
    for i in range(1 if first else 0, groups):
        for part in range(2):
            for copy in half_copies(i, part):
                copy.wait()
    if plan.got:
        for copy in got_copies:
            copy.wait()


def chunk_call(plan, norm, counts, nodes_in, cotangent, halo, weights, carry, gacc, fulls, got):
    vmem = pl.BlockSpec(memory_space=pltpu.VMEM)
    hbm = pl.BlockSpec(memory_space=pltpu.HBM)
    either = pl.BlockSpec(memory_space=pl.ANY)
    slab = nodes_in.shape[0]
    groups, first, grads_on = plan.groups, plan.first, not plan.beyond
    buffer = HALO + groups * GROUP
    sds = jax.ShapeDtypeStruct
    weight_shapes = [(256, 768), (768, 256), (256, 256), (256, 256)]
    aliases = {}
    if first:
        args = [counts, nodes_in, cotangent, halo] + list(weights)
        in_specs = [hbm] * 3 + [either] * 3
    else:
        args = [counts, nodes_in, cotangent] + list(weights) + list(carry) + ([gacc] if grads_on else []) + list(fulls)
        in_specs = [hbm] * 3 + [either] * (len(args) - 5) + [hbm] * 2
        aliases = {len(args) - 2: 0, len(args) - 1: 1}
    if got is not None:
        args.append(got)
        in_specs.append(either)
    out_shape = [sds((slab, 128), BF), sds((slab, 128), BF)]
    if plan.send:
        out_shape.append(sds((plan.rows, 256), BF))
    out_specs = [hbm] * 2 + [either] * (len(out_shape) - 2)
    if first:
        out_shape += [sds(shape, BF) for shape in weight_shapes]
        out_specs += [vmem] * 4
    if plan.carry:
        out_shape += [sds((HALO, 512), BF)] * 3
        out_specs += [either] * 3
    if grads_on:
        out_shape.append(sds((2, 1024, 128), BF) if plan.last else sds((256, 1024), F32))
        out_specs.append(vmem if plan.last else either)
    scratch = [
        pltpu.VMEM((buffer, 256), BF),
        pltpu.VMEM((buffer, 256), BF),
        pltpu.VMEM((buffer, 512), BF),
        pltpu.VMEM((buffer, 512), BF),
        pltpu.VMEM((buffer, 512), BF),
        pltpu.VMEM((2, 4, GROUP, 128), F32),
        pltpu.VMEM((4, GROUP, 128), F32),
        pltpu.VMEM((256, 1024), F32),
        pltpu.VMEM((256, 1024), F32),
        pltpu.VMEM((buffer, 128), BF),
        pltpu.VMEM((buffer, 128), BF),
        pltpu.VMEM((buffer, 256), BF),
        pltpu.SMEM((counts.shape[0],), jnp.int32),
        pltpu.SemaphoreType.DMA((2 * groups + 1, 2)),
        pltpu.SemaphoreType.DMA((9,)),
        pltpu.SemaphoreType.DMA((groups, 6)),
    ]
    if first:
        scratch += [pltpu.VMEM((1024, 128), BF)] * 2
    else:
        scratch += [pltpu.VMEM(shape, BF) for shape in weight_shapes]
    if got is not None:
        scratch += [pltpu.VMEM(got.shape, BF), pltpu.SemaphoreType.DMA((3,))]
    outs = pl.pallas_call(
        functools.partial(chunk_kernel, plan, norm),
        out_shape=out_shape,
        in_specs=in_specs,
        out_specs=out_specs,
        input_output_aliases=aliases,
        scratch_shapes=scratch,
        compiler_params=pltpu.CompilerParams(vmem_limit_bytes=VMEM_LIMIT),
        cost_estimate=pl.CostEstimate(
            flops=plan.rows * plan.cost, bytes_accessed=plan.rows * 1000, transcendentals=0
        ),
    )(*args)
    outs = list(outs)
    fulls, rest = outs[:2], outs[2:]
    sent = rest.pop(0) if plan.send else None
    if first:
        weights, rest = rest[:4], rest[4:]
    carry, rest = (rest[:3], rest[3:]) if plan.carry else (None, rest)
    gacc = rest[0] if grads_on else None
    return fulls, sent, weights, carry, gacc


def pack_kernel(x_hbm, c_hbm, wq, wk, wv, wo, packed, rims, stage, sems):
    side = lax.axis_index("head").astype(jnp.int32)
    rows = pl.ds(pl.multiple_of((1 - side) * (x_hbm.shape[0] - HALO), HALO), HALO)
    loads = [
        pltpu.make_async_copy(x_hbm.at[rows], rims.at[:, pl.ds(0, 256)], sems.at[0]),
        pltpu.make_async_copy(c_hbm.at[rows], rims.at[:, pl.ds(256, 256)], sems.at[1]),
        pltpu.make_async_copy(wq, packed.at[pl.ds(0, 256)], sems.at[2]),
        pltpu.make_async_copy(wk, packed.at[pl.ds(256, 256)], sems.at[3]),
        pltpu.make_async_copy(wv, packed.at[pl.ds(512, 256)], sems.at[4]),
        pltpu.make_async_copy(wo, stage, sems.at[5]),
    ]
    for copy in loads:
        copy.start()
    for copy in loads:
        copy.wait()
    packed[768:896, :] = stage[:, 0:128]
    packed[896:1024, :] = stage[:, 128:256]


def pack_call(nodes_in, cotangent, w_query, w_key, w_value, w_out):
    vmem = pl.BlockSpec(memory_space=pltpu.VMEM)
    hbm = pl.BlockSpec(memory_space=pltpu.HBM)
    return pl.pallas_call(
        pack_kernel,
        out_shape=(jax.ShapeDtypeStruct((1024, 128), BF), jax.ShapeDtypeStruct((HALO, 512), BF)),
        in_specs=[hbm] * 6,
        out_specs=(vmem, vmem),
        scratch_shapes=[pltpu.VMEM(w_out.shape, BF), pltpu.SemaphoreType.DMA((6,))],
    )(nodes_in, cotangent, w_query, w_key, w_value, w_out)


def per_device(nodes_in, cotangent, w_query, w_key, w_value, w_out, counts):
    row_count = nodes_in.shape[0]
    gz, heads, tiles = lax.axis_size("gz"), lax.axis_size("head"), lax.axis_size("tile")
    places = gz * tiles
    swap = [(0, 1), (1, 0)]

    def flat(p, h):
        return (p // tiles * heads + h) * tiles + p % tiles

    own, rims = pack_call(nodes_in, cotangent, w_query, w_key, w_value, w_out)
    oth = lax.ppermute(own, "head", swap)
    route = [(flat(p, 0), flat((p + 1) % places, 0)) for p in range(places)]
    route += [(flat(p, 1), flat((p - 1) % places, 1)) for p in range(places)]
    halo = lax.ppermute(rims, ("gz", "head", "tile"), route)

    norm = float(row_count * places) ** (-0.5)
    weights, carry, gacc, fulls = (own, oth), None, None, None
    waiting, first_group, row = [], 0, 0
    own_count, beyond_count = len(OWN_CALLS), len(BEYOND_CALLS)

    for n, groups in enumerate(OWN_CALLS + BEYOND_CALLS):
        first, beyond = n == 0, n >= own_count
        last, end = n == own_count - 1, n == own_count + beyond_count - 1
        send = n < own_count - 1
        got_rows, got = waiting.pop(0) if waiting and n > 1 else (None, None)
        spot = None if got is None else (got_rows, got.shape[0])
        plan = Plan(first_group, groups, first, last, beyond, send, not end, spot)
        fulls, sent, weights, carry, gacc = chunk_call(
            plan, norm, counts, nodes_in, cotangent, halo, weights, carry, gacc, fulls, got
        )
        if send:
            waiting.append((row, lax.ppermute(sent, "head", swap)))
        if last:
            grads = gacc.reshape(heads * places, 1024 // places, 128)
            grads = lax.all_to_all(grads, ("head", "gz", "tile"), 0, 0, tiled=True)
        if n == own_count:
            grads, *fulls = lax.optimization_barrier((grads, *fulls))
        first_group += groups
        row += plan.rows

    share = jnp.sum(grads.astype(F32), axis=0).astype(BF)
    share = jnp.broadcast_to(share[None], (places,) + share.shape)
    whole = lax.all_to_all(share, ("gz", "tile"), 0, 0, tiled=True).reshape(1024, 128).astype(F32)
    grad_out = whole[768:1024].reshape(16, 2, 8, 128).transpose(0, 2, 1, 3).reshape(128, 256)
    return (fulls[0], fulls[1], whole[0:256], whole[256:512], whole[512:768], grad_out)


def solution(mesh):
    return jax.shard_map(
        per_device,
        mesh=mesh,
        in_specs=(
            P(("gz", "tile"), None),
            P(("gz", "tile"), None),
            P(None, "head"),
            P(None, "head"),
            P(None, "head"),
            P("head", None),
            P(),
        ),
        out_specs=(
            P(("gz", "tile"), "head"),
            P(("gz", "tile"), "head"),
            P(None, "head"),
            P(None, "head"),
            P(None, "head"),
            P("head", None),
        ),
        check_vma=False,
    )
```
